32 devices in a mesh: gx: 8 (over y, x, core), gy: 4 (over z).
Axes of the slice: x: 2, y: 2, z: 4, core: 2. Of those that a mesh axis runs over, the one named last changes fastest.
Arguments:
- density: float32 [2, 32, 512], P(None, 'gx', 'gy'), may hold values from 0 to 1
- e_field: float32 [3, 32, 32, 512], P(None, 'gx', None, 'gy'), may hold values from -6 to 6
- h_field: float32 [3, 32, 32, 512], P(None, 'gx', None, 'gy'), may hold values from -6 to 6
- adj_e: float32 [3, 32, 32, 512], P(None, 'gx', None, 'gy'), may hold values from -6 to 6
- adj_h: float32 [3, 32, 32, 512], P(None, 'gx', None, 'gy'), may hold values from -6 to 6
- region: int32 [32, 512], P('gx', 'gy'), may hold values from 0 to 3
Outputs:
- density_grad: float32 [2, 32, 512], P(None, 'gx', 'gy')
- adj_e0: float32 [3, 32, 32, 512], P(None, 'gx', None, 'gy')
- adj_h0: float32 [3, 32, 32, 512], P(None, 'gx', None, 'gy')
The draws below stay inside these ranges and needn't reach their ends.
Inputs may be any that keep to these rules, and one draw needn't show every extreme that they name: `region`: 0 open, 1 absorbing, 2 design, 3 source.
All inputs are finite; a program needn't handle non-finite values.
Results may differ from the reference program's by a relative error of at most 0.00002.
Values sent between devices are 32-bit elements; how exact they have to be, the bound alone decides.
No kernel may reach another device: no remote copies, remote signals or barrier semaphores. Data moves between devices by JAX's collectives and lax.ppermute only.
A program may use at most 64 MiB of HBM per device.

```python
import math
import jax
import jax.numpy as jnp
import numpy as np
from jax import lax

NZ = 32
RAD = 2
STEPS = 2
NX = 32
NY = 512


def place_ends(array, rng, least, largest):
    extent = array.shape
    index_at = [jax.random.randint(jax.random.fold_in(rng, axis), (), 0, extent[axis]) for axis in range(len(extent))]
    array = array.at[tuple(index_at)].set(least)
    longest = extent.index(max(extent))
    index_at[longest] = (index_at[longest] + 1) % extent[longest]
    return array.at[tuple(index_at)].set(largest)


def shard_levels(rng, dims, pieces, smallest, top_value):
    gain = 1.0
    for axis_at, blocks in pieces:
        heights = jax.random.uniform(jax.random.fold_in(jax.random.fold_in(rng, 6), axis_at), (blocks,), jnp.float32, smallest / len(pieces), top_value / len(pieces))
        gain = gain * jnp.repeat(jnp.exp(heights), dims[axis_at] // blocks).reshape((-1,) + (1,) * (len(dims) - 1 - axis_at))
    return gain


def normal_values(rng, shape, deviation, bound, pieces=(), dtype=jnp.bfloat16):
    values = deviation * jax.random.normal(rng, shape, jnp.float32)
    if pieces:
        values = values * shard_levels(rng, shape, pieces, -0.22, 0.18)
    return jnp.clip(values, -bound, bound).astype(dtype)


def setup_inputs(seed: int = 0) -> dict:
    arg_keys = jax.random.split(jax.random.key(seed), 7)
    return {
        "density": jnp.clip(1.0 * jax.random.uniform(arg_keys[0], (2, NX, NY), jnp.float32) ** shard_levels(arg_keys[0], (2, NX, NY), ((1, 8), (2, 4)), -0.2, 0.2), 0.0, 1.0),
        "e_field": normal_values(arg_keys[1], (3, NX, NZ, NY), 1.0, 6.0, ((1, 8), (3, 4)), jnp.float32),
        "h_field": normal_values(arg_keys[2], (3, NX, NZ, NY), 1.0, 6.0, ((1, 8), (3, 4)), jnp.float32),
        "adj_e": normal_values(arg_keys[3], (3, NX, NZ, NY), 1.0, 6.0, ((1, 8), (3, 4)), jnp.float32),
        "adj_h": normal_values(arg_keys[4], (3, NX, NZ, NY), 1.0, 6.0, ((1, 8), (3, 4)), jnp.float32),
        "region": place_ends(jax.random.randint(arg_keys[5], (NX, NY), 0, 4), jax.random.fold_in(arg_keys[5], 1), 0, 3).astype(jnp.int32),
    }


COURANT = 0.5
SHARP = 4.0
LEVEL = 0.5
CONTRAST = 5.0
ABSORB = 0.3
OMEGA = 0.7

def kernel_table(radius):
    offsets = np.arange(-radius, radius + 1)
    distance = np.sqrt(offsets[:, None] ** 2 + offsets[None, :] ** 2)
    table = np.maximum(0.0, radius + 1.0 - distance)
    return table / table.sum()

def conic_blur(padded, width_x, width_y, radius):
    table = kernel_table(radius)
    total = jnp.zeros((padded.shape[0], width_x, width_y), jnp.float32)
    for row_off in range(2 * radius + 1):
        for col_off in range(2 * radius + 1):
            total = total + float(table[row_off, col_off]) * padded[:, row_off:row_off + width_x, col_off:col_off + width_y]
    return total

def project(filtered):
    crest = math.tanh(SHARP * LEVEL)
    return (crest + jnp.tanh(SHARP * (filtered - LEVEL))) / (crest + math.tanh(SHARP * (1.0 - LEVEL)))

def coefficients(projected, region, slab_depth):
    depth_pos = jnp.arange(slab_depth).astype(jnp.float32)
    margin = float(slab_depth // 8)
    centre = slab_depth // 2
    ramp_z = jnp.maximum(jnp.maximum((margin - depth_pos) / margin, (depth_pos - (slab_depth - 1 - margin)) / margin), 0.0)
    design = (region == 2).astype(jnp.float32)
    absorbing = (region == 1).astype(jnp.float32)
    layer_zero = (jnp.arange(slab_depth) == centre).astype(jnp.float32)
    layer_one = (jnp.arange(slab_depth) == centre + 1).astype(jnp.float32)
    permit = 1.0 + CONTRAST * design[:, None, :] * (projected[0][:, None, :] * layer_zero[None, :, None] + projected[1][:, None, :] * layer_one[None, :, None])
    damping = ABSORB * absorbing[:, None, :] + ABSORB * (ramp_z * ramp_z)[None, :, None]
    keep_e = (1.0 - damping) / (1.0 + damping)
    gain_e = COURANT / (permit * (1.0 + damping))
    return (keep_e, gain_e, permit)

def source(region, slab_depth, step):
    columns = (region == 3).astype(jnp.float32)
    source_plane = (jnp.arange(slab_depth) == slab_depth // 2 - 1).astype(jnp.float32)
    along_z = math.sin(OMEGA * (step + 1)) * columns[:, None, :] * source_plane[None, :, None]
    return jnp.stack([jnp.zeros_like(along_z), jnp.zeros_like(along_z), along_z])

def diff_up(values, along):
    count = values.shape[along]
    following = jnp.concatenate([lax.slice_in_dim(values, 1, count, axis=along), jnp.zeros_like(lax.slice_in_dim(values, 0, 1, axis=along))], along)
    return following - values

def diff_down(values, along):
    count = values.shape[along]
    preceding = jnp.concatenate([jnp.zeros_like(lax.slice_in_dim(values, 0, 1, axis=along)), lax.slice_in_dim(values, 0, count - 1, axis=along)], along)
    return values - preceding

def curl_of(field, differ):
    part_x, part_y, part_z = (field[0], field[1], field[2])
    return jnp.stack([differ(part_z, 2) - differ(part_y, 1), differ(part_x, 1) - differ(part_z, 0), differ(part_y, 0) - differ(part_x, 2)])

def forward(density, e_field, h_field, region):
    padded = jnp.pad(density, ((0, 0), (RAD, RAD), (RAD, RAD)))
    projected = project(conic_blur(padded, density.shape[1], density.shape[2], RAD))
    keep_e, gain_e, permit = coefficients(projected, region, e_field.shape[2])
    elec, magn = (e_field, h_field)
    for step in range(STEPS):
        magn = magn - COURANT * curl_of(elec, diff_up)
        drive = curl_of(magn, diff_down) - source(region, e_field.shape[2], step)
        elec = keep_e * elec + gain_e * drive
    return (elec, magn)

def reference(density, e_field, h_field, adj_e, adj_h, region):

    def mapping(dens, elec, magn):
        return forward(dens, elec, magn, region)
    outputs, pullback = jax.vjp(mapping, density, e_field, h_field)
    gradients = pullback((adj_e, adj_h))
    return (gradients[0], gradients[1], gradients[2])
```

```python
import functools
import math

import jax
import jax.numpy as jnp
import numpy as np
from jax import lax
from jax.experimental import pallas as pl
from jax.experimental.pallas import tpu as pltpu
from jax.sharding import PartitionSpec as P

RAD = 2
COURANT = 0.5
SHARP = 4.0
LEVEL = 0.5
CONTRAST = 5.0
ABSORB = 0.3
OMEGA = 0.7
CREST = math.tanh(SHARP * LEVEL)
SCALE = CREST + math.tanh(SHARP * (1.0 - LEVEL))

LANES = 128
TILE = 8
FULL_K = 2
WIN_K = 4
DEN_K = 8
FIRST, LAST = -4, 8
DEN_BASE = 6


def kernel_table(radius):
    offsets = np.arange(-radius, radius + 1)
    distance = np.sqrt(offsets[:, None] ** 2 + offsets[None, :] ** 2)
    table = np.maximum(0.0, radius + 1.0 - distance)
    return table / table.sum()


def odd_swap(index):
    return ((index + 1) ^ 1) - 1


def pair_permute(block, partner):
    count_x, count_y = lax.axis_size("gx"), lax.axis_size("gy")
    route = []
    for i in range(count_x):
        for j in range(count_y):
            a, b = partner(i, j, count_x, count_y)
            route.append((i * count_y + j, a * count_y + b))
    return lax.ppermute(block, ("gx", "gy"), route)


def x_even(i, j, nx, ny):
    return i ^ 1, j


def x_odd(i, j, nx, ny):
    return (odd_swap(i), j) if 0 < i < nx - 1 else (i, j ^ 1)


def y_even(i, j, nx, ny):
    return i, j ^ 1


def y_odd(i, j, nx, ny):
    return (i, odd_swap(j)) if 0 < j < ny - 1 else (i ^ 1, j)


def x_far_low(i, j, nx, ny):
    return (i + 2 if i % 4 < 2 else i - 2), j


def x_far_high(i, j, nx, ny):
    a = i + 2 if i % 4 >= 2 else i - 2
    return (a, j) if 0 <= a < nx else (i ^ 1, j)


class Sent:
    def __init__(self, depth):
        self.depth = depth
        self.full = {}
        at = 0
        for name in ("ae", "ah"):
            for c in range(3):
                for near in range(2):
                    self.full[name, c, near] = at
                    at += depth
        self.third = {}
        for name in ("ae", "ah"):
            for c in range(3):
                self.third[name, c] = at
                at += TILE
        self.window = {}
        for name in ("e", "h"):
            for c in range(3):
                for row in range(4):
                    self.window[name, c, row] = at
                    at += TILE
        self.density = at
        at += TILE
        self.region = at
        at += TILE
        self.rows = at


class Packed:
    def __init__(self, depth):
        self.full = {}
        slots = LANES // (2 * FULL_K)
        count = 0
        for name in ("ae", "ah"):
            for c in range(3):
                for row in range(-2, 6):
                    self.full[name, c, row] = (count // slots * depth, count % slots)
                    count += 1
        at = -(-count // slots) * depth
        self.full_rows = at
        self.window = {}
        slots = LANES // (2 * WIN_K)
        count = 0
        for name, low, high in (("e", FIRST, LAST), ("h", FIRST, LAST), ("ae", -3, 7), ("ah", -3, 7)):
            for c in range(3):
                for row in range(low, high):
                    self.window[name, c, row] = (at + count // slots * TILE, count % slots)
                    count += 1
        at += -(-count // slots) * TILE
        self.window_rows = at
        self.density = at
        self.rows = at + TILE


def lane_index(rows, lanes=LANES):
    return lax.broadcasted_iota(jnp.int32, (rows, lanes), 1)


def pack_x_kernel(depth, den, e, h, ae, ah, reg, to_even, to_odd):
    odd = lax.rem(lax.axis_index("gx"), 2)
    sent = Sent(depth)
    rows = den.shape[1]
    low = depth // 2 - 4
    for ref, right in ((to_even, 1 - odd), (to_odd, odd)):
        start = right * (rows - 2)
        third = 2 + right * (rows - 5)
        for name, field in (("ae", ae), ("ah", ah)):
            for c in range(3):
                for near in range(2):
                    at = sent.full[name, c, near]
                    ref[at : at + depth, :] = field[c, start + near]
                at = sent.third[name, c]
                ref[at : at + TILE, :] = field[c, third, low : low + TILE, :]
        for name, field in (("e", e), ("h", h)):
            for c in range(3):
                for row in range(4):
                    at = sent.window[name, c, row]
                    ref[at : at + TILE, :] = field[c, row, low : low + TILE, :]
        at = sent.density
        ref[at : at + 4, :] = den[0]
        ref[at + 4 : at + 8, :] = den[1]
        at = sent.region
        ref[at : at + 4, :] = reg[...].astype(jnp.float32)
        ref[at + 4 : at + 8, :] = jnp.zeros((4, LANES), jnp.float32)


class Rows:
    def __init__(self, depth, own, from_even, from_odd):
        index = lax.axis_index("gx")
        last = lax.axis_size("gx") - 1
        odd = lax.rem(index, 2)
        even = 1 - odd
        as_float = lambda flag: flag.astype(jnp.float32)
        self.left = as_float(odd), as_float(even * (index > 0).astype(jnp.int32))
        self.right = as_float(even), as_float(odd * (index < last).astype(jnp.int32))
        self.sent = Sent(depth)
        self.depth = depth
        self.low = depth // 2 - 4
        self.own = own
        self.even, self.odd = from_even, from_odd

    def of(self, side, at, count):
        return side[0] * self.even[at : at + count, :] + side[1] * self.odd[at : at + count, :]

    def full(self, name, c, row):
        if 0 <= row < 4:
            return self.own[name][c, row]
        if row < 0:
            return self.of(self.left, self.sent.full[name, c, row + 2], self.depth)
        return self.of(self.right, self.sent.full[name, c, row - 4], self.depth)

    def window(self, name, c, row):
        low, sent = self.low, self.sent
        if 0 <= row < 4:
            return self.own[name][c, row, low : low + TILE, :]
        side = self.left if row < 0 else self.right
        if name in ("e", "h"):
            return self.of(side, sent.window[name, c, row + 4 if row < 0 else row - 4], TILE)
        if row in (-3, 6):
            return self.of(side, sent.third[name, c], TILE)
        return self.of(side, sent.full[name, c, row + 2 if row < 0 else row - 4] + low, TILE)


def pack_y_kernel(depth, den, e, h, ae, ah, reg, from_even, from_odd, far_low, far_high, packed, columns):
    rows = Rows(depth, {"e": e, "h": h, "ae": ae, "ah": ah}, from_even, from_odd)
    plan = Packed(depth)
    index = lax.axis_index("gx")
    last = lax.axis_size("gx") - 1
    high = lax.rem(index, 4) // 2
    as_float = lambda flag: flag.astype(jnp.float32)
    left_far = as_float(high), as_float((1 - high) * (index > 1).astype(jnp.int32))
    right_far = as_float(1 - high), as_float(high * (index < last - 1).astype(jnp.int32))
    zero_row = jnp.zeros((1, LANES), jnp.float32)
    left = rows.of(rows.left, rows.sent.density, TILE)
    right = rows.of(rows.right, rows.sent.density, TILE)
    for layer in range(2):
        at = layer * 16
        columns[at : at + 1, :] = zero_row
        columns[at + 1 : at + 2, :] = left_far[0] * far_low[layer, 3:4, :] + left_far[1] * far_high[layer, 3:4, :]
        columns[at + 2 : at + 6, :] = left[4 * layer : 4 * layer + 4]
        columns[at + 6 : at + 10, :] = den[layer]
        columns[at + 10 : at + 14, :] = right[4 * layer : 4 * layer + 4]
        columns[at + 14 : at + 15, :] = right_far[0] * far_low[layer, 0:1, :] + right_far[1] * far_high[layer, 0:1, :]
        columns[at + 15 : at + 16, :] = zero_row
    at = 32
    columns[at : at + 2, :] = jnp.zeros((2, LANES), jnp.float32)
    columns[at + 2 : at + 6, :] = rows.of(rows.left, rows.sent.region, TILE)[:4]
    columns[at + 6 : at + 10, :] = reg[...].astype(jnp.float32)
    columns[at + 10 : at + 14, :] = rows.of(rows.right, rows.sent.region, TILE)[:4]
    columns[at + 14 : at + 16, :] = jnp.zeros((2, LANES), jnp.float32)

    def pack(planes, width, count):
        slots = LANES // (2 * width)
        owner = lax.rem((lane_index(count) + width) // (2 * width), slots)
        total = None
        for slot, plane in enumerate(planes):
            moved = pltpu.roll(plane, slot * 2 * width, 1) if slot else plane
            total = moved if total is None else jnp.where(owner == slot, moved, total)
        return total

    groups = {}
    for key, (at, slot) in plan.full.items():
        groups.setdefault(at, []).append(key)
    for at, keys in groups.items():
        packed[at : at + depth, :] = pack([rows.full(*key) for key in keys], FULL_K, depth)
    groups = {}
    for key, (at, slot) in plan.window.items():
        groups.setdefault(at, []).append(key)
    for at, keys in groups.items():
        packed[at : at + TILE, :] = pack([rows.window(*key) for key in keys], WIN_K, TILE)
    at = plan.density
    packed[at : at + TILE, :] = pack([columns[8 * n : 8 * n + 8, :] for n in range(6)], DEN_K, TILE)


def up_z(block):
    depth = block.shape[0]
    moved = pltpu.roll(block, depth - 1, 0)
    if depth == TILE:
        return moved - block
    edge = lax.broadcasted_iota(jnp.int32, block.shape, 0) == depth - 1
    return jnp.where(edge, 0.0, moved) - block


def down_z(block):
    moved = pltpu.roll(block, 1, 0)
    if block.shape[0] == TILE:
        return block - moved
    edge = lax.broadcasted_iota(jnp.int32, block.shape, 0) == 0
    return block - jnp.where(edge, 0.0, moved)


def up_y(block):
    return pltpu.roll(block, block.shape[1] - 1, 1) - block


def down_y(block):
    return block - pltpu.roll(block, 1, 1)


def curl_up(here, after):
    x, y, z = here
    return (up_y(z) - up_z(y), up_z(x) - (after[2] - z), (after[1] - y) - up_y(x))


def curl_down(here, before):
    x, y, z = here
    return (down_y(z) - down_z(y), down_z(x) - (z - before[2]), (y - before[1]) - down_y(x))


def blur(block):
    table = kernel_table(RAD)
    lanes, count = block.shape[1], block.shape[0]
    sums = [block]
    for b in range(1, RAD + 1):
        sums.append(pltpu.roll(block, b, 1) + pltpu.roll(block, lanes - b, 1))
    total = None
    for a in range(RAD + 1):
        part = sum(float(table[RAD + a, RAD + b]) * sums[b] for b in range(RAD + 1))
        if a:
            part = pltpu.roll(part, a, 0) + pltpu.roll(part, count - a, 0)
        total = part if total is None else total + part
    return total


def main_kernel(
    depth, den, e, h, ae, ah, reg, from_even, from_odd, columns, packed_even, packed_odd,
    grad, out_e, out_h,
    halo, ga, bh, be, gb, ratio_rows,
):
    rows = Rows(depth, {"e": e, "h": h, "ae": ae, "ah": ah}, from_even, from_odd)
    plan = Packed(depth)
    wide = 2 * LANES
    centre = depth // 2
    low = rows.low
    j = lax.axis_index("gy")
    last_y = lax.axis_size("gy") - 1
    odd_y = lax.rem(j, 2)
    even_y = 1 - odd_y
    as_float = lambda flag: flag.astype(jnp.float32)
    has_left = as_float((j > 0).astype(jnp.int32))
    has_right = as_float((j < last_y).astype(jnp.int32))
    left = as_float(odd_y), as_float(even_y * (j > 0).astype(jnp.int32))
    right = as_float(even_y), as_float(odd_y * (j < last_y).astype(jnp.int32))

    def combine(at, count, width):
        from_left = lax.rem(lane_index(count), 2 * width) >= width
        even, odd = packed_even[at : at + count, :], packed_odd[at : at + count, :]
        halo[at : at + count, :] = jnp.where(from_left, left[0] * even + left[1] * odd, right[0] * even + right[1] * odd)

    combine(0, plan.full_rows, FULL_K)
    combine(plan.full_rows, plan.window_rows - plan.full_rows, WIN_K)
    combine(plan.density, TILE, DEN_K)

    def unroll(at, count, shift):
        block = halo[at : at + count, :]
        return pltpu.roll(block, LANES - shift, 1) if shift else block

    def full(name, c, row):
        at, slot = plan.full[name, c, row]
        return jnp.concatenate([rows.full(name, c, row), unroll(at, depth, slot * 2 * FULL_K)], 1)

    def window(name, c, row):
        at, slot = plan.window[name, c, row]
        return jnp.concatenate([rows.window(name, c, row), unroll(at, TILE, slot * 2 * WIN_K)], 1)

    def column_block(n):
        parts = []
        for half in range(2):
            at = 8 * (2 * n + half)
            parts.append(
                jnp.concatenate(
                    [columns[at : at + 8, :], unroll(plan.density, TILE, (2 * n + half) * 2 * DEN_K)], 1
                )
            )
        return jnp.concatenate(parts, 0)

    region = column_block(2)
    design = (region == 2.0).astype(jnp.float32)
    absorbing = (region == 1.0).astype(jnp.float32)
    source = (region == 3.0).astype(jnp.float32)
    inverse, slope = [], []
    for layer in range(2):
        inner = jnp.tanh(SHARP * (blur(column_block(layer)) - LEVEL))
        projected = (CREST + inner) / SCALE
        slope.append(SHARP * (1.0 - inner * inner) / SCALE)
        inverse.append(1.0 / (1.0 + CONTRAST * design * projected))
    damp = ABSORB * absorbing
    keep_col = (1.0 - damp) / (1.0 + damp)
    gain_col = COURANT / (1.0 + damp)

    lane = lane_index(TILE, wide)
    inside = jnp.where(lane < LANES, 1.0, jnp.where(lane < LANES + LANES // 2, has_right, has_left))
    has_below = rows.left[0] + rows.left[1]
    has_above = rows.right[0] + rows.right[1]
    masks = {"own": inside, "below": inside * has_below, "above": inside * has_above}
    steps = {key: COURANT * value for key, value in masks.items()}
    where_row = lambda row: "own" if 0 <= row < 4 else ("below" if row < 0 else "above")

    def spread(block, row, count=TILE):
        at = row + DEN_BASE
        return jnp.broadcast_to(block[at : at + 1, :], (count, block.shape[1]))

    sub = lax.broadcasted_iota(jnp.int32, (TILE, wide), 0) + low

    def layered(row):
        first, second = spread(inverse[0], row), spread(inverse[1], row)
        return jnp.where(sub == centre, first, jnp.where(sub == centre + 1, second, 1.0))

    keep_win = {row: spread(keep_col, row) for row in range(-3, 7)}
    layer_win = {row: layered(row) for row in range(-3, 7)}
    gain_win = {row: spread(gain_col, row) * layer_win[row] * masks[where_row(row)] for row in range(-3, 7)}
    source_plane = (sub == centre - 1).astype(jnp.float32)
    amounts = [math.sin(OMEGA * (step + 1)) for step in range(2)]
    e0 = {row: [window("e", c, row) for c in range(3)] for row in range(-4, 8)}
    h0 = {row: [window("h", c, row) for c in range(3)] for row in range(-4, 7)}
    h1, e1, h2, drive1, drive2 = {}, {}, {}, {}, {}

    def minus_step(base, curl, row):
        step = steps[where_row(row)]
        return [b - step * c for b, c in zip(base, curl)]

    for row in range(-4, 7):
        h1[row] = minus_step(h0[row], curl_up(e0[row], e0[row + 1]), row)
    for row in range(-3, 7):
        drive = list(curl_down(h1[row], h1[row - 1]))
        at_source = source_plane * spread(source, row)
        drive[2] = drive[2] - amounts[0] * at_source
        drive1[row] = drive
        e1[row] = [keep_win[row] * b + gain_win[row] * d for b, d in zip(e0[row], drive)]
    for row in range(-3, 6):
        h2[row] = minus_step(h1[row], curl_up(e1[row], e1[row + 1]), row)
    for row in range(-2, 6):
        drive2[row] = list(curl_down(h2[row], h2[row - 1]))
        drive2[row][2] = drive2[row][2] - amounts[1] * source_plane * spread(source, row)
    a2 = {row: [window("ae", c, row) for c in range(3)] for row in range(-3, 7)}
    ga_win = {row: [gain_win[row] * v for v in a2[row]] for row in range(-3, 7)}
    bh_win = {}
    for row in range(-3, 6):
        mask = masks[where_row(row)]
        curl = curl_up(ga_win[row], ga_win[row + 1])
        bh_win[row] = [window("ah", c, row) + mask * curl[c] for c in range(3)]
    ratio_rows[...] = jnp.zeros(ratio_rows.shape, jnp.float32)
    for row in range(-2, 6):
        a1 = minus_step(
            [keep_win[row] * v for v in a2[row]], curl_down(bh_win[row], bh_win[row - 1]), row
        )
        total = sum(a2[row][c] * drive2[row][c] + a1[c] * drive1[row][c] for c in range(3))
        for layer in range(2):
            at = centre + layer - low
            ratio_rows[layer, row + DEN_BASE : row + DEN_BASE + 1, :] = total[at : at + 1, :]
    for layer in range(2):
        sensitivity = -ratio_rows[layer] * gain_col * inverse[layer] * inverse[layer]
        smoothed = blur(CONTRAST * design * sensitivity * slope[layer])
        grad[layer] = smoothed[DEN_BASE : DEN_BASE + 4, :LANES]

    z = lax.broadcasted_iota(jnp.int32, (depth, wide), 0)
    zf = z.astype(jnp.float32)
    margin = float(depth // 8)
    ramp = jnp.maximum(jnp.maximum((margin - zf) / margin, (zf - (depth - 1 - margin)) / margin), 0.0)
    open_damp = ABSORB * ramp * ramp
    full_damp = open_damp + ABSORB
    gain_open, gain_abs = COURANT / (1.0 + open_damp), COURANT / (1.0 + full_damp)
    keep_open, keep_abs = (1.0 - open_damp) / (1.0 + open_damp), (1.0 - full_damp) / (1.0 + full_damp)

    def coefficient(row):
        flag = spread(absorbing, row, depth) > 0.5
        layers = jnp.where(
            z == centre,
            spread(inverse[0], row, depth),
            jnp.where(z == centre + 1, spread(inverse[1], row, depth), 1.0),
        )
        return jnp.where(flag, keep_abs, keep_open), jnp.where(flag, gain_abs, gain_open) * layers

    def stretch(block):
        return jnp.broadcast_to(block[:1, :], (depth, wide))

    masks = {key: stretch(value) for key, value in masks.items()}
    steps = {key: stretch(value) for key, value in steps.items()}

    for row in range(-2, 6):
        keep, gain = coefficient(row)
        for c in range(3):
            value = full("ae", c, row)
            ga[c, row + 2] = gain * value
            if -1 <= row <= 4:
                be[c, row + 1] = keep * value
    for row in range(-2, 5):
        curl = curl_up([ga[c, row + 2] for c in range(3)], [ga[c, row + 3] for c in range(3)])
        for c in range(3):
            bh[c, row + 2] = full("ah", c, row) + masks[where_row(row)] * curl[c]
    for row in range(-1, 5):
        keep, gain = coefficient(row)
        curl = curl_down([bh[c, row + 2] for c in range(3)], [bh[c, row + 1] for c in range(3)])
        for c in range(3):
            value = be[c, row + 1] - steps[where_row(row)] * curl[c]
            be[c, row + 1] = keep * value
            gb[c, row + 1] = gain * value
    for row in range(-1, 4):
        curl = curl_up([gb[c, row + 1] for c in range(3)], [gb[c, row + 2] for c in range(3)])
        for c in range(3):
            value = bh[c, row + 2] + masks[where_row(row)] * curl[c]
            bh[c, row + 2] = value
            if row >= 0:
                out_h[c, row] = value[:, :LANES]
    for row in range(4):
        curl = curl_down([bh[c, row + 2] for c in range(3)], [bh[c, row + 1] for c in range(3)])
        for c in range(3):
            out_e[c, row] = be[c, row + 1][:, :LANES] - COURANT * curl[c][:, :LANES]


def per_device(density, e_field, h_field, adj_e, adj_h, region):
    depth = e_field.shape[2]
    sent, plan = Sent(depth), Packed(depth)
    f32 = jnp.float32
    own = (density, e_field, h_field, adj_e, adj_h, region)
    params = pltpu.CompilerParams(vmem_limit_bytes=32 * 1024 * 1024)
    shape = jax.ShapeDtypeStruct
    to_even, to_odd = pl.pallas_call(
        functools.partial(pack_x_kernel, depth),
        out_shape=(shape((sent.rows, LANES), f32),) * 2,
        compiler_params=params,
        name="pack_x",
    )(*own)
    from_odd = pair_permute(to_odd, x_odd)
    from_even = pair_permute(to_even, x_even)
    far_low = pair_permute(density, x_far_low)
    far_high = pair_permute(density, x_far_high)
    packed, columns = pl.pallas_call(
        functools.partial(pack_y_kernel, depth),
        out_shape=(shape((plan.rows, LANES), f32), shape((48, LANES), f32)),
        compiler_params=params,
        name="pack_y",
    )(*own, from_even, from_odd, far_low, far_high)
    packed_odd = pair_permute(packed, y_odd)
    packed_even = pair_permute(packed, y_even)
    wide = 2 * LANES
    return pl.pallas_call(
        functools.partial(main_kernel, depth),
        out_shape=(
            shape(density.shape, f32),
            shape(e_field.shape, f32),
            shape(e_field.shape, f32),
        ),
        scratch_shapes=[
            pltpu.VMEM((plan.rows, LANES), f32),
            pltpu.VMEM((3, 8, depth, wide), f32),
            pltpu.VMEM((3, 7, depth, wide), f32),
            pltpu.VMEM((3, 6, depth, wide), f32),
            pltpu.VMEM((3, 6, depth, wide), f32),
            pltpu.VMEM((2, 16, wide), f32),
        ],
        compiler_params=params,
        name="adjoint",
    )(*own, from_even, from_odd, columns, packed_even, packed_odd)


def solution(mesh):
    field = P(None, "gx", None, "gy")
    design = P(None, "gx", "gy")
    return jax.shard_map(
        per_device,
        mesh=mesh,
        in_specs=(design, field, field, field, field, P("gx", "gy")),
        out_specs=(design, field, field),
        check_vma=False,
    )
```

```python
import functools
import math

import jax
import jax.numpy as jnp
import numpy as np
from jax import lax
from jax.experimental import pallas as pl
from jax.experimental.pallas import tpu as pltpu
from jax.sharding import PartitionSpec as P

RAD = 2
COURANT = 0.5
SHARP = 4.0
LEVEL = 0.5
CONTRAST = 5.0
ABSORB = 0.3
OMEGA = 0.7
CREST = math.tanh(SHARP * LEVEL)
SCALE = CREST + math.tanh(SHARP * (1.0 - LEVEL))

LANES = 128
LOAD_VMEM = 56 * 1024 * 1024
TILE = 8
FULL_K = 2
WIN_K = 4
FIRST, LAST = -4, 8
DEN_BASE = 6


def kernel_table(radius):
    offsets = np.arange(-radius, radius + 1)
    distance = np.sqrt(offsets[:, None] ** 2 + offsets[None, :] ** 2)
    table = np.maximum(0.0, radius + 1.0 - distance)
    return table / table.sum()


def odd_swap(index):
    return ((index + 1) ^ 1) - 1


def pair_permute(block, partner):
    count_x, count_y = lax.axis_size("gx"), lax.axis_size("gy")
    route = []
    for i in range(count_x):
        for j in range(count_y):
            a, b = partner(i, j, count_x, count_y)
            route.append((i * count_y + j, a * count_y + b))
    return lax.ppermute(block, ("gx", "gy"), route)


def x_even(i, j, nx, ny):
    return i ^ 1, j


def x_odd(i, j, nx, ny):
    return (odd_swap(i), j) if 0 < i < nx - 1 else (i, j ^ 1)


def x_ring(i, j, nx, ny):
    return odd_swap(i) % nx, j


def y_even(i, j, nx, ny):
    return i, j ^ 1


def y_odd(i, j, nx, ny):
    return (i, odd_swap(j)) if 0 < j < ny - 1 else (i ^ 1, j)


class Sent:
    def __init__(self, depth):
        self.full = {}
        at = 0
        for name in ("ae", "ah"):
            for c in range(3):
                for near in range(2):
                    self.full[name, c, near] = at
                    at += depth
        self.third = {}
        for name in ("ae", "ah"):
            for c in range(3):
                self.third[name, c] = at
                at += TILE
        self.window = {}
        for name in ("e", "h"):
            for c in range(3):
                for row in range(4):
                    self.window[name, c, row] = at
                    at += TILE
        self.density = at
        self.region = at + TILE
        self.mate = at + 2 * TILE
        self.rows = at + 3 * TILE


FIELDS = ("ae", "ah", "e", "h")


class Edges:
    def __init__(self, depth):
        self.window_at = depth
        self.columns_at = depth + 3 * TILE
        self.mate_at = self.columns_at + 2 * TILE
        self.rows = self.mate_at + TILE

    def full_slot(self, name, c, row):
        return row % 4 * 6 + FIELDS.index(name) * 3 + c

    def window_slot(self, name, c, row):
        place = (FIELDS.index(name) * 3 + c) * 4 + row % 4
        return place // 16 * TILE, place % 16


def lane_index(rows, lanes=LANES):
    return lax.broadcasted_iota(jnp.int32, (rows, lanes), 1)


def pack(planes, width):
    slots = LANES // (2 * width)
    owner = lax.rem((lane_index(planes[0].shape[0]) + width) // (2 * width), slots)
    total = None
    for slot, plane in enumerate(planes):
        moved = pltpu.roll(plane, slot * 2 * width, 1) if slot else plane
        total = moved if total is None else jnp.where(owner == slot, moved, total)
    return total


def near_layers(depth):
    low = depth // 2 - 4
    return low, low // TILE * TILE


def load_kernel(depth, den, e, h, ae, ah, reg, own_den, own_e, own_h, own_ae, own_ah, own_reg, sems):
    near = pl.ds(near_layers(depth)[1], 2 * TILE)
    pairs = (
        (ae, own_ae),
        (ah, own_ah),
        (e.at[:, :, near, :], own_e),
        (h.at[:, :, near, :], own_h),
        (den, own_den),
        (reg, own_reg),
    )
    copies = [pltpu.make_async_copy(source, target, sems.at[n]) for n, (source, target) in enumerate(pairs)]
    for copy in copies:
        copy.start()
    for copy in copies:
        copy.wait()


def near_windows(depth, e, h, ae, ah):
    low, base = near_layers(depth)
    windows = []
    for field, start in ((ae, low), (ah, low), (e, low - base), (h, low - base)):
        for c in range(3):
            for row in range(4):
                windows.append(field[c, row, start : start + TILE, :])
    return windows


def first_kernel(depth, den, e, h, ae, ah, reg, mate_den, edges, to_even, to_odd):
    plan, sent = Edges(depth), Sent(depth)
    low = near_layers(depth)[0]
    odd = lax.rem(lax.axis_index("gx"), 2)
    own = {"ae": ae, "ah": ah}
    windows = near_windows(depth, e, h, ae, ah)
    for ref, right in ((to_even, 1 - odd), (to_odd, odd)):
        start = right * (ae.shape[1] - 2)
        third = 2 + right * (ae.shape[1] - 5)
        for name in ("ae", "ah"):
            for c in range(3):
                for near in range(2):
                    at = sent.full[name, c, near]
                    ref[at : at + depth, :] = own[name][c, start + near]
                at = sent.third[name, c]
                ref[at : at + TILE, :] = own[name][c, third, low : low + TILE, :]
        for n, name in ((2, "e"), (3, "h")):
            for c in range(3):
                for row in range(4):
                    at = sent.window[name, c, row]
                    ref[at : at + TILE, :] = windows[(3 * n + c) * 4 + row]
    planes = [own[name][c, row] for row in range(4) for name in ("ae", "ah") for c in range(3)]
    edges[0:depth, :] = pack(planes, FULL_K)
    for n in range(3):
        at = plan.window_at + n * TILE
        edges[at : at + TILE, :] = pack(windows[16 * n : 16 * n + 16], WIN_K)
    for ref, at, mate in (
        (edges, plan.columns_at, plan.mate_at),
        (to_even, sent.density, sent.mate),
        (to_odd, sent.density, sent.mate),
    ):
        ref[at : at + 4, :] = den[0]
        ref[at + 4 : at + 8, :] = den[1]
        ref[at + 8 : at + 12, :] = reg[...].astype(jnp.float32)
        ref[at + 12 : at + 16, :] = jnp.zeros((4, LANES), jnp.float32)
        ref[mate : mate + 4, :] = mate_den[0]
        ref[mate + 4 : mate + 8, :] = mate_den[1]


def as_float(flag):
    return flag.astype(jnp.float32)


class Sides:
    def __init__(self, axis):
        index = lax.axis_index(axis)
        last = lax.axis_size(axis) - 1
        odd = lax.rem(index, 2)
        even = 1 - odd
        self.left = as_float(odd), as_float(even * (index > 0).astype(jnp.int32))
        self.right = as_float(even), as_float(odd * (index < last).astype(jnp.int32))

    @staticmethod
    def of(side, even, odd, at, count):
        return side[0] * even[at : at + count, :] + side[1] * odd[at : at + count, :]


class Rows:
    def __init__(self, depth, own, from_even, from_odd):
        self.sides = Sides("gx")
        self.sent = Sent(depth)
        self.depth = depth
        self.low, self.base = near_layers(depth)
        self.own = own
        self.even, self.odd = from_even, from_odd

    def of(self, row, at, count):
        side = self.sides.left if row < 0 else self.sides.right
        return self.sides.of(side, self.even, self.odd, at, count)

    def full(self, name, c, row):
        if 0 <= row < 4:
            return self.own[name][c, row]
        return self.of(row, self.sent.full[name, c, row + 2 if row < 0 else row - 4], self.depth)

    def window(self, name, c, row):
        sent = self.sent
        if 0 <= row < 4:
            low = self.low - self.base if name in ("e", "h") else self.low
            return self.own[name][c, row, low : low + TILE, :]
        if name in ("e", "h"):
            return self.of(row, sent.window[name, c, row % 4], TILE)
        if row in (-3, 6):
            return self.of(row, sent.third[name, c], TILE)
        return self.of(row, sent.full[name, c, row + 2 if row < 0 else row - 4] + self.low, TILE)


def combine_kernel(depth, even, odd, halo):
    plan = Edges(depth)
    sides = Sides("gy")
    for at, end, width in (
        (0, plan.window_at, FULL_K),
        (plan.window_at, plan.columns_at, WIN_K),
        (plan.columns_at, plan.rows, LANES // 2),
    ):
        from_left = lax.rem(lane_index(end - at), 2 * width) >= width
        left = sides.of(sides.left, even, odd, at, end - at)
        right = sides.of(sides.right, even, odd, at, end - at)
        halo[at:end, :] = jnp.where(from_left, left, right)


def columns_kernel(depth, den, reg, from_even, from_odd, halo, halo_even, halo_odd, columns, far):
    plan, sent = Edges(depth), Sent(depth)
    sides = Sides("gx")
    odd = as_float(lax.rem(lax.axis_index("gx"), 2))
    for lane, (own, even, away, at, mate) in enumerate(
        (
            (None, from_even, from_odd, sent.density, sent.mate),
            (halo, halo_even, halo_odd, plan.columns_at, plan.mate_at),
        )
    ):
        lanes = pl.ds(lane * LANES, LANES)
        below = sides.of(sides.left, even, away, at, 2 * TILE)
        above = sides.of(sides.right, even, away, at, 2 * TILE)
        zero_row = jnp.zeros((1, LANES), jnp.float32)
        for n in range(3):
            if own is None:
                here = den[n] if n < 2 else reg[...].astype(jnp.float32)
            else:
                here = own[at + 4 * n : at + 4 * n + 4, :]
            to = 16 * n
            columns[to : to + 1, lanes] = zero_row
            columns[to + 15 : to + 16, lanes] = zero_row
            first = last = zero_row
            if n < 2:
                first = sides.left[1] * away[mate + 4 * n + 3 : mate + 4 * n + 4, :]
                last = sides.right[1] * away[mate + 4 * n : mate + 4 * n + 1, :]
                far[2 * n + lane : 2 * n + lane + 1, :] = (1.0 - odd) * below[4 * n + 3 : 4 * n + 4] + odd * above[4 * n : 4 * n + 1]
            columns[to + 1 : to + 2, lanes] = first
            columns[to + 2 : to + 6, lanes] = below[4 * n : 4 * n + 4]
            columns[to + 6 : to + 10, lanes] = here
            columns[to + 10 : to + 14, lanes] = above[4 * n : 4 * n + 4]
            columns[to + 14 : to + 15, lanes] = last
    far[4:8, :] = jnp.zeros((4, LANES), jnp.float32)


def up_z(block):
    depth = block.shape[0]
    moved = pltpu.roll(block, depth - 1, 0)
    if depth == TILE:
        return moved - block
    edge = lax.broadcasted_iota(jnp.int32, block.shape, 0) == depth - 1
    return jnp.where(edge, 0.0, moved) - block


def down_z(block):
    moved = pltpu.roll(block, 1, 0)
    if block.shape[0] == TILE:
        return block - moved
    edge = lax.broadcasted_iota(jnp.int32, block.shape, 0) == 0
    return block - jnp.where(edge, 0.0, moved)


def up_y(block):
    return pltpu.roll(block, block.shape[1] - 1, 1) - block


def down_y(block):
    return block - pltpu.roll(block, 1, 1)


def curl_up(here, after):
    x, y, z = here
    return (up_y(z) - up_z(y), up_z(x) - (after[2] - z), (after[1] - y) - up_y(x))


def curl_down(here, before):
    x, y, z = here
    return (down_y(z) - down_z(y), down_z(x) - (z - before[2]), (y - before[1]) - down_y(x))


def blur(block):
    table = kernel_table(RAD)
    lanes, count = block.shape[1], block.shape[0]
    sums = [block]
    for b in range(1, RAD + 1):
        sums.append(pltpu.roll(block, b, 1) + pltpu.roll(block, lanes - b, 1))
    total = None
    for a in range(RAD + 1):
        part = sum(float(table[RAD + a, RAD + b]) * sums[b] for b in range(RAD + 1))
        if a:
            part = pltpu.roll(part, a, 0) + pltpu.roll(part, count - a, 0)
        total = part if total is None else total + part
    return total


class Halos:
    def __init__(self, depth, x_sides, own, even, odd):
        self.depth = depth
        self.plan = Edges(depth)
        self.x_sides = x_sides
        self.own, self.even, self.odd = own, even, odd

    def of(self, row, at, count):
        if 0 <= row < 4:
            return self.own[at : at + count, :]
        side = self.x_sides.left if row < 0 else self.x_sides.right
        return self.x_sides.of(side, self.even, self.odd, at, count)

    def full(self, name, c, row):
        return unroll(self.of(row, 0, self.depth), self.plan.full_slot(name, c, row) * 2 * FULL_K)

    def window(self, name, c, row):
        at, slot = self.plan.window_slot(name, c, row)
        return unroll(self.of(row, self.plan.window_at + at, TILE), slot * 2 * WIN_K)


def unroll(block, shift):
    return pltpu.roll(block, LANES - shift, 1) if shift else block


class Coefficients:
    def __init__(self, region, densities):
        self.design = (region == 2.0).astype(jnp.float32)
        self.absorbing = (region == 1.0).astype(jnp.float32)
        self.source = (region == 3.0).astype(jnp.float32)
        self.inverse, self.slope = [], []
        for density in densities:
            inner = jnp.tanh(SHARP * (blur(density) - LEVEL))
            projected = (CREST + inner) / SCALE
            self.slope.append(SHARP * (1.0 - inner * inner) / SCALE)
            self.inverse.append(1.0 / (1.0 + CONTRAST * self.design * projected))
        damp = ABSORB * self.absorbing
        self.keep = (1.0 - damp) / (1.0 + damp)
        self.gain = COURANT / (1.0 + damp)


def inside_masks(x_sides, y_sides):
    lane = lane_index(TILE, 2 * LANES)
    inside = jnp.where(lane < LANES, 1.0, jnp.where(lane < LANES + LANES // 2, sum(y_sides.right), sum(y_sides.left)))
    return {"own": inside, "below": inside * sum(x_sides.left), "above": inside * sum(x_sides.right)}


def where_row(row):
    return "own" if 0 <= row < 4 else ("below" if row < 0 else "above")


def spread(block, row, count=TILE):
    at = row + DEN_BASE
    return jnp.broadcast_to(block[at : at + 1, :], (count, block.shape[1]))


def near_kernel(
    depth, e, h, ae, ah, from_even, from_odd, halo, halo_even, halo_odd, columns, far,
    grad,
    ratio_rows,
):
    rows = Rows(depth, {"e": e, "h": h, "ae": ae, "ah": ah}, from_even, from_odd)
    halos = Halos(depth, rows.sides, halo, halo_even, halo_odd)
    wide = 2 * LANES
    centre = depth // 2
    low = rows.low

    def window(name, c, row):
        return jnp.concatenate([rows.window(name, c, row), halos.window(name, c, row)], 1)

    odd = lax.rem(lax.axis_index("gx"), 2)
    far_at = jnp.where(odd == 1, DEN_BASE - 5, DEN_BASE + 8)
    at_far = lax.broadcasted_iota(jnp.int32, (16, wide), 0) == far_at
    densities = []
    for layer in range(2):
        row = jnp.concatenate([far[2 * layer : 2 * layer + 1, :], far[2 * layer + 1 : 2 * layer + 2, :]], 1)
        densities.append(jnp.where(at_far, jnp.broadcast_to(row, (16, wide)), columns[16 * layer : 16 * layer + 16, :]))
    known = Coefficients(columns[32:48, :], densities)
    inverse, slope, design, source = known.inverse, known.slope, known.design, known.source
    keep_col, gain_col = known.keep, known.gain
    masks = inside_masks(rows.sides, Sides("gy"))
    steps = {key: COURANT * value for key, value in masks.items()}

    sub = lax.broadcasted_iota(jnp.int32, (TILE, wide), 0) + low

    def layered(row):
        first, second = spread(inverse[0], row), spread(inverse[1], row)
        return jnp.where(sub == centre, first, jnp.where(sub == centre + 1, second, 1.0))

    keep_win = {row: spread(keep_col, row) for row in range(-3, 7)}
    layer_win = {row: layered(row) for row in range(-3, 7)}
    gain_win = {row: spread(gain_col, row) * layer_win[row] * masks[where_row(row)] for row in range(-3, 7)}
    source_plane = (sub == centre - 1).astype(jnp.float32)
    amounts = [math.sin(OMEGA * (step + 1)) for step in range(2)]
    e0 = {row: [window("e", c, row) for c in range(3)] for row in range(-4, 8)}
    h0 = {row: [window("h", c, row) for c in range(3)] for row in range(-4, 7)}
    h1, e1, h2, drive1, drive2 = {}, {}, {}, {}, {}

    def minus_step(base, curl, row):
        step = steps[where_row(row)]
        return [b - step * c for b, c in zip(base, curl)]

    for row in range(-4, 7):
        h1[row] = minus_step(h0[row], curl_up(e0[row], e0[row + 1]), row)
    for row in range(-3, 7):
        drive = list(curl_down(h1[row], h1[row - 1]))
        at_source = source_plane * spread(source, row)
        drive[2] = drive[2] - amounts[0] * at_source
        drive1[row] = drive
        e1[row] = [keep_win[row] * b + gain_win[row] * d for b, d in zip(e0[row], drive)]
    for row in range(-3, 6):
        h2[row] = minus_step(h1[row], curl_up(e1[row], e1[row + 1]), row)
    for row in range(-2, 6):
        drive2[row] = list(curl_down(h2[row], h2[row - 1]))
        drive2[row][2] = drive2[row][2] - amounts[1] * source_plane * spread(source, row)
    a2 = {row: [window("ae", c, row) for c in range(3)] for row in range(-3, 7)}
    ga_win = {row: [gain_win[row] * v for v in a2[row]] for row in range(-3, 7)}
    bh_win = {}
    for row in range(-3, 6):
        mask = masks[where_row(row)]
        curl = curl_up(ga_win[row], ga_win[row + 1])
        bh_win[row] = [window("ah", c, row) + mask * curl[c] for c in range(3)]
    ratio_rows[...] = jnp.zeros(ratio_rows.shape, jnp.float32)
    for row in range(-2, 6):
        a1 = minus_step(
            [keep_win[row] * v for v in a2[row]], curl_down(bh_win[row], bh_win[row - 1]), row
        )
        total = sum(a2[row][c] * drive2[row][c] + a1[c] * drive1[row][c] for c in range(3))
        for layer in range(2):
            at = centre + layer - low
            ratio_rows[layer, row + DEN_BASE : row + DEN_BASE + 1, :] = total[at : at + 1, :]
    for layer in range(2):
        sensitivity = -ratio_rows[layer] * gain_col * inverse[layer] * inverse[layer]
        smoothed = blur(CONTRAST * design * sensitivity * slope[layer])
        grad[layer] = smoothed[DEN_BASE : DEN_BASE + 4, :LANES]


def full_kernel(
    depth, ae, ah, from_even, from_odd, halo, halo_even, halo_odd, columns,
    out_e, out_h,
    ga, bh, be, gb,
):
    rows = Rows(depth, {"ae": ae, "ah": ah}, from_even, from_odd)
    halos = Halos(depth, rows.sides, halo, halo_even, halo_odd)
    wide = 2 * LANES
    centre = depth // 2

    def full(name, c, row):
        return jnp.concatenate([rows.full(name, c, row), halos.full(name, c, row)], 1)

    known = Coefficients(columns[32:48, :], [columns[16 * layer : 16 * layer + 16, :] for layer in range(2)])
    inverse, absorbing = known.inverse, known.absorbing
    masks = inside_masks(rows.sides, Sides("gy"))
    steps = {key: COURANT * value for key, value in masks.items()}

    z = lax.broadcasted_iota(jnp.int32, (depth, wide), 0)
    zf = z.astype(jnp.float32)
    margin = float(depth // 8)
    ramp = jnp.maximum(jnp.maximum((margin - zf) / margin, (zf - (depth - 1 - margin)) / margin), 0.0)
    open_damp = ABSORB * ramp * ramp
    full_damp = open_damp + ABSORB
    gain_open, gain_abs = COURANT / (1.0 + open_damp), COURANT / (1.0 + full_damp)
    keep_open, keep_abs = (1.0 - open_damp) / (1.0 + open_damp), (1.0 - full_damp) / (1.0 + full_damp)

    def coefficient(row):
        flag = spread(absorbing, row, depth) > 0.5
        layers = jnp.where(
            z == centre,
            spread(inverse[0], row, depth),
            jnp.where(z == centre + 1, spread(inverse[1], row, depth), 1.0),
        )
        return jnp.where(flag, keep_abs, keep_open), jnp.where(flag, gain_abs, gain_open) * layers

    def stretch(block):
        return jnp.broadcast_to(block[:1, :], (depth, wide))

    masks = {key: stretch(value) for key, value in masks.items()}
    steps = {key: stretch(value) for key, value in steps.items()}

    for row in range(-2, 6):
        keep, gain = coefficient(row)
        for c in range(3):
            value = full("ae", c, row)
            ga[c, row + 2] = gain * value
            if -1 <= row <= 4:
                be[c, row + 1] = keep * value
    for row in range(-2, 5):
        curl = curl_up([ga[c, row + 2] for c in range(3)], [ga[c, row + 3] for c in range(3)])
        for c in range(3):
            bh[c, row + 2] = full("ah", c, row) + masks[where_row(row)] * curl[c]
    for row in range(-1, 5):
        keep, gain = coefficient(row)
        curl = curl_down([bh[c, row + 2] for c in range(3)], [bh[c, row + 1] for c in range(3)])
        for c in range(3):
            value = be[c, row + 1] - steps[where_row(row)] * curl[c]
            be[c, row + 1] = keep * value
            gb[c, row + 1] = gain * value
    for row in range(-1, 4):
        curl = curl_up([gb[c, row + 1] for c in range(3)], [gb[c, row + 2] for c in range(3)])
        for c in range(3):
            value = bh[c, row + 2] + masks[where_row(row)] * curl[c]
            bh[c, row + 2] = value
            if row >= 0:
                out_h[c, row] = value[:, :LANES]
    for row in range(4):
        curl = curl_down([bh[c, row + 2] for c in range(3)], [bh[c, row + 1] for c in range(3)])
        for c in range(3):
            out_e[c, row] = be[c, row + 1][:, :LANES] - COURANT * curl[c][:, :LANES]


def per_device(density, e_field, h_field, adj_e, adj_h, region):
    depth = e_field.shape[2]
    sent, plan = Sent(depth), Edges(depth)
    f32 = jnp.float32
    params = pltpu.CompilerParams(vmem_limit_bytes=32 * 1024 * 1024)
    shape = jax.ShapeDtypeStruct
    near = e_field.shape[:2] + (2 * TILE, LANES)
    mate_den = pair_permute(density, x_even)
    own = pl.pallas_call(
        functools.partial(load_kernel, depth),
        out_shape=(
            pltpu.VMEM(density.shape, f32),
            pltpu.VMEM(near, f32),
            pltpu.VMEM(near, f32),
            pltpu.VMEM(adj_e.shape, f32),
            pltpu.VMEM(adj_h.shape, f32),
            pltpu.VMEM(region.shape, region.dtype),
        ),
        in_specs=[pl.BlockSpec(memory_space=pltpu.HBM)] * 6,
        scratch_shapes=[pltpu.SemaphoreType.DMA((6,))],
        compiler_params=pltpu.CompilerParams(vmem_limit_bytes=LOAD_VMEM),
        name="load",
    )(density, e_field, h_field, adj_e, adj_h, region)
    fields = own[1:5]
    edges, to_even, to_odd = pl.pallas_call(
        functools.partial(first_kernel, depth),
        out_shape=(
            shape((plan.rows, LANES), f32),
            shape((sent.rows, LANES), f32),
            shape((sent.rows, LANES), f32),
        ),
        compiler_params=params,
        name="first",
    )(*own, mate_den)
    edges_odd = pair_permute(edges, y_odd)
    edges_even = pair_permute(edges, y_even)
    from_odd = pair_permute(to_odd, x_ring)
    from_even = pair_permute(to_even, x_even)
    halo = pl.pallas_call(
        functools.partial(combine_kernel, depth),
        out_shape=shape((plan.rows, LANES), f32),
        compiler_params=params,
        name="combine",
    )(edges_even, edges_odd)
    halo_odd = pair_permute(halo, x_odd)
    halo_even = pair_permute(halo, x_even)
    wide = 2 * LANES
    columns, far = pl.pallas_call(
        functools.partial(columns_kernel, depth),
        out_shape=(shape((48, wide), f32), shape((TILE, LANES), f32)),
        compiler_params=params,
        name="columns",
    )(own[0], own[5], from_even, from_odd, halo, halo_even, halo_odd)
    far = pair_permute(far, x_even)
    adj_e0, adj_h0 = pl.pallas_call(
        functools.partial(full_kernel, depth),
        out_shape=(shape(e_field.shape, f32), shape(e_field.shape, f32)),
        scratch_shapes=[
            pltpu.VMEM((3, 8, depth, wide), f32),
            pltpu.VMEM((3, 7, depth, wide), f32),
            pltpu.VMEM((3, 6, depth, wide), f32),
            pltpu.VMEM((3, 6, depth, wide), f32),
        ],
        compiler_params=params,
        name="full",
    )(*fields[2:], from_even, from_odd, halo, halo_even, halo_odd, columns)
    grad = pl.pallas_call(
        functools.partial(near_kernel, depth),
        out_shape=shape(density.shape, f32),
        scratch_shapes=[pltpu.VMEM((2, 16, wide), f32)],
        compiler_params=params,
        name="near",
    )(*fields, from_even, from_odd, halo, halo_even, halo_odd, columns, far)
    return grad, adj_e0, adj_h0


def solution(mesh):
    field = P(None, "gx", None, "gy")
    design = P(None, "gx", "gy")
    return jax.shard_map(
        per_device,
        mesh=mesh,
        in_specs=(design, field, field, field, field, P("gx", "gy")),
        out_specs=(design, field, field),
        check_vma=False,
    )
```

```python
import functools
import math

import jax
import jax.numpy as jnp
import numpy as np
from jax import lax
from jax.experimental import pallas as pl
from jax.experimental.pallas import tpu as pltpu
from jax.sharding import PartitionSpec as P

RAD = 2
COURANT = 0.5
SHARP = 4.0
LEVEL = 0.5
CONTRAST = 5.0
ABSORB = 0.3
OMEGA = 0.7
CREST = math.tanh(SHARP * LEVEL)
SCALE = CREST + math.tanh(SHARP * (1.0 - LEVEL))

LANES = 128
LOAD_VMEM = 56 * 1024 * 1024
TILE = 8
FULL_K = 2
WIN_K = 4
FIRST, LAST = -4, 8
DEN_BASE = 6


def kernel_table(radius):
    offsets = np.arange(-radius, radius + 1)
    distance = np.sqrt(offsets[:, None] ** 2 + offsets[None, :] ** 2)
    table = np.maximum(0.0, radius + 1.0 - distance)
    return table / table.sum()


def odd_swap(index):
    return ((index + 1) ^ 1) - 1


def pair_permute(block, partner):
    count_x, count_y = lax.axis_size("gx"), lax.axis_size("gy")
    route = []
    for i in range(count_x):
        for j in range(count_y):
            a, b = partner(i, j, count_x, count_y)
            route.append((i * count_y + j, a * count_y + b))
    return lax.ppermute(block, ("gx", "gy"), route)


def x_even(i, j, nx, ny):
    return i ^ 1, j


def x_odd(i, j, nx, ny):
    return (odd_swap(i), j) if 0 < i < nx - 1 else (i, j ^ 1)


def x_ring(i, j, nx, ny):
    return odd_swap(i) % nx, j


def y_even(i, j, nx, ny):
    return i, j ^ 1


def y_odd(i, j, nx, ny):
    return (i, odd_swap(j)) if 0 < j < ny - 1 else (i ^ 1, j)


PIECES = (
    ("e", 1, (0, 1, 2), 6, -2, -2),
    ("e", 2, (0, 1, 2), 6, -2, -2),
    ("e", 3, (0, 1, 2), 5, -1, -2),
    ("e", 4, (0, 1, 2), 4, 0, -2),
    ("h", 1, (0, 1, 2), 5, -2, -2),
    ("h", 2, (0, 1, 2), 5, -2, -2),
    ("h", 3, (0, 1, 2), 4, -1, -2),
    ("h", 4, (1, 2), 3, 0, 0),
    ("ae", 3, (0, 1, 2), 3, 0, -1),
    ("ah", 3, (1, 2), 2, 0, 0),
    ("ah", 2, (0,), 3, -1, -1),
)


class Sent:
    def __init__(self, depth):
        self.full = {}
        at = 0
        for name, far in (("ae", (0, 1, 2)), ("ah", (1, 2))):
            for distance in (1, 2):
                for c in (0, 1, 2) if distance == 1 else far:
                    self.full[name, c, distance] = at
                    at += depth
        self.pieces = {}
        for name, distance, components, count, left, right in PIECES:
            for c in components:
                self.pieces[name, c, distance] = at, count, left, right
                at += count
        at = -(-at // TILE) * TILE
        self.density = at
        self.region = at + TILE
        self.mate = at + 2 * TILE
        self.rows = at + 3 * TILE


FIELDS = ("ae", "ah", "e", "h")


COLUMN_K = 8
COLUMN_LANE = 104


class Edges:
    def __init__(self, depth):
        self.window_at = depth
        self.rows = depth + 3 * TILE
        self.density, self.region, self.mate = 0, TILE, 2 * TILE

    def full_slot(self, name, c, row):
        return row % 4 * 6 + FIELDS.index(name) * 3 + c

    def window_slot(self, name, c, row):
        place = (FIELDS.index(name) * 3 + c) * 4 + row % 4
        return place // 16 * TILE, place % 16


def lane_index(rows, lanes=LANES):
    return lax.broadcasted_iota(jnp.int32, (rows, lanes), 1)


def pack(planes, width):
    slots = LANES // (2 * width)
    owner = lax.rem((lane_index(planes[0].shape[0]) + width) // (2 * width), slots)
    total = None
    for slot, plane in enumerate(planes):
        moved = pltpu.roll(plane, slot * 2 * width, 1) if slot else plane
        total = moved if total is None else jnp.where(owner == slot, moved, total)
    return total


def near_layers(depth):
    low = depth // 2 - 4
    return low, low // TILE * TILE


def load_kernel(depth, den, e, h, ae, ah, reg, own_den, own_e, own_h, own_ae, own_ah, own_reg, sems):
    near = pl.ds(near_layers(depth)[1], 2 * TILE)
    pairs = (
        (ae, own_ae),
        (ah, own_ah),
        (e.at[:, :, near, :], own_e),
        (h.at[:, :, near, :], own_h),
        (den, own_den),
        (reg, own_reg),
    )
    copies = [pltpu.make_async_copy(source, target, sems.at[n]) for n, (source, target) in enumerate(pairs)]
    for copy in copies:
        copy.start()
    for copy in copies:
        copy.wait()


def near_windows(depth, e, h, ae, ah):
    low, base = near_layers(depth)
    windows = []
    for field, start in ((ae, low), (ah, low), (e, low - base), (h, low - base)):
        for c in range(3):
            for row in range(4):
                windows.append(field[c, row, start : start + TILE, :])
    return windows


def first_kernel(depth, den, e, h, ae, ah, reg, mate_den, edges, to_even, to_odd):
    plan, sent = Edges(depth), Sent(depth)
    low = near_layers(depth)[0]
    odd = lax.rem(lax.axis_index("gx"), 2)
    own = {"ae": ae, "ah": ah}
    windows = near_windows(depth, e, h, ae, ah)
    centre = depth // 2
    base = near_layers(depth)[1]
    fields = {"ae": (ae, centre), "ah": (ah, centre), "e": (e, centre - base), "h": (h, centre - base)}
    for ref, right in ((to_even, 1 - odd), (to_odd, odd)):
        row_of = lambda distance: right * (ae.shape[1] + 1 - 2 * distance) + distance - 1
        for (name, c, distance), at in sent.full.items():
            ref[at : at + depth, :] = own[name][c, row_of(distance)]
        for (name, c, distance), (at, count, from_left, from_right) in sent.pieces.items():
            field, middle = fields[name]
            row = row_of(distance)
            value = field[c, row, middle + from_left : middle + from_left + count, :]
            if from_left != from_right:
                other = field[c, row, middle + from_right : middle + from_right + count, :]
                value = jnp.where(jnp.full(value.shape, right, jnp.int32) == 1, value, other)
            ref[at : at + count, :] = value
    planes = [own[name][c, row] for row in range(4) for name in ("ae", "ah") for c in range(3)]
    blank = jnp.zeros((4, LANES), jnp.float32)
    column = jnp.concatenate(
        [den[0], den[1], reg[...].astype(jnp.float32), blank, mate_den[0], mate_den[1]]
        + [blank] * ((depth - 3 * TILE) // 4),
        0,
    )
    lane = lane_index(depth)
    mine = (lane >= COLUMN_LANE - COLUMN_K) & (lane < COLUMN_LANE + COLUMN_K)
    edges[0:depth, :] = jnp.where(mine, pltpu.roll(column, COLUMN_LANE, 1), pack(planes, FULL_K))
    for n in range(3):
        at = plan.window_at + n * TILE
        edges[at : at + TILE, :] = pack(windows[16 * n : 16 * n + 16], WIN_K)
    for ref in (to_even, to_odd):
        at = sent.density
        ref[at : at + 3 * TILE, :] = column[: 3 * TILE]


def as_float(flag):
    return flag.astype(jnp.float32)


class Sides:
    def __init__(self, axis):
        index = lax.axis_index(axis)
        last = lax.axis_size(axis) - 1
        odd = lax.rem(index, 2)
        even = 1 - odd
        self.left = as_float(odd), as_float(even * (index > 0).astype(jnp.int32))
        self.right = as_float(even), as_float(odd * (index < last).astype(jnp.int32))

    @staticmethod
    def of(side, even, odd, at, count):
        return side[0] * even[at : at + count, :] + side[1] * odd[at : at + count, :]


class Rows:
    def __init__(self, depth, own, from_even, from_odd):
        self.sides = Sides("gx")
        self.sent = Sent(depth)
        self.depth = depth
        self.low, self.base = near_layers(depth)
        self.own = own
        self.even, self.odd = from_even, from_odd

    def of(self, row, at, count):
        side = self.sides.left if row < 0 else self.sides.right
        return self.sides.of(side, self.even, self.odd, at, count)

    def full(self, name, c, row):
        if 0 <= row < 4:
            return self.own[name][c, row]
        distance = -row if row < 0 else row - 3
        if (name, c, distance) not in self.sent.full:
            return jnp.zeros((self.depth, LANES), jnp.float32)
        return self.of(row, self.sent.full[name, c, distance], self.depth)

    def window(self, name, c, row):
        sent = self.sent
        if 0 <= row < 4:
            low = self.low - self.base if name in ("e", "h") else self.low
            return self.own[name][c, row, low : low + TILE, :]
        distance = -row if row < 0 else row - 3
        if (name, c, distance) in sent.full:
            return self.of(row, sent.full[name, c, distance] + self.low, TILE)
        if (name, c, distance) not in sent.pieces:
            return jnp.zeros((TILE, LANES), jnp.float32)
        at, count, from_left, from_right = sent.pieces[name, c, distance]
        at -= self.depth // 2 - self.low + (from_left if row < 0 else from_right)
        return self.of(row, at, TILE)


def combine_kernel(depth, even, odd, halo):
    plan = Edges(depth)
    sides = Sides("gy")
    for at, end, width in ((0, plan.window_at, FULL_K), (plan.window_at, plan.rows, WIN_K)):
        lane = lane_index(end - at)
        from_left = lax.rem(lane, 2 * width) >= width
        if at == 0:
            beside = (lane >= COLUMN_LANE - COLUMN_K) & (lane < COLUMN_LANE + COLUMN_K)
            from_left = jnp.where(beside, (lane < COLUMN_LANE).astype(jnp.int32), from_left.astype(jnp.int32)) == 1
        left = sides.of(sides.left, even, odd, at, end - at)
        right = sides.of(sides.right, even, odd, at, end - at)
        halo[at:end, :] = jnp.where(from_left, left, right)


def columns_kernel(depth, den, reg, from_even, from_odd, halo, halo_even, halo_odd, columns, far):
    sent = Sent(depth)
    sides = Sides("gx")
    odd = as_float(lax.rem(lax.axis_index("gx"), 2))
    count = 3 * TILE

    def beside(ref):
        return pltpu.roll(ref[0:count, :], LANES - COLUMN_LANE, 1)

    def within(ref):
        return ref[sent.density : sent.density + count, :]

    for lane, (own, even, away) in enumerate(
        ((None, within(from_even), within(from_odd)), (beside(halo), beside(halo_even), beside(halo_odd)))
    ):
        lanes = pl.ds(lane * LANES, LANES)
        below = sides.left[0] * even + sides.left[1] * away
        above = sides.right[0] * even + sides.right[1] * away
        zero_row = jnp.zeros((1, LANES), jnp.float32)
        mate = 2 * TILE
        for n in range(3):
            if own is None:
                here = den[n] if n < 2 else reg[...].astype(jnp.float32)
            else:
                here = own[4 * n : 4 * n + 4]
            to = 16 * n
            columns[to : to + 1, lanes] = zero_row
            columns[to + 15 : to + 16, lanes] = zero_row
            first = last = zero_row
            if n < 2:
                first = sides.left[1] * away[mate + 4 * n + 3 : mate + 4 * n + 4]
                last = sides.right[1] * away[mate + 4 * n : mate + 4 * n + 1]
                far[2 * n + lane : 2 * n + lane + 1, :] = (1.0 - odd) * below[4 * n + 3 : 4 * n + 4] + odd * above[4 * n : 4 * n + 1]
            columns[to + 1 : to + 2, lanes] = first
            columns[to + 2 : to + 6, lanes] = below[4 * n : 4 * n + 4]
            columns[to + 6 : to + 10, lanes] = here
            columns[to + 10 : to + 14, lanes] = above[4 * n : 4 * n + 4]
            columns[to + 14 : to + 15, lanes] = last
    far[4:8, :] = jnp.zeros((4, LANES), jnp.float32)


def up_z(block):
    depth = block.shape[0]
    moved = pltpu.roll(block, depth - 1, 0)
    if depth == TILE:
        return moved - block
    edge = lax.broadcasted_iota(jnp.int32, block.shape, 0) == depth - 1
    return jnp.where(edge, 0.0, moved) - block


def down_z(block):
    moved = pltpu.roll(block, 1, 0)
    if block.shape[0] == TILE:
        return block - moved
    edge = lax.broadcasted_iota(jnp.int32, block.shape, 0) == 0
    return block - jnp.where(edge, 0.0, moved)


def up_y(block):
    return pltpu.roll(block, block.shape[1] - 1, 1) - block


def down_y(block):
    return block - pltpu.roll(block, 1, 1)


def curl_up(here, after):
    x, y, z = here
    return (up_y(z) - up_z(y), up_z(x) - (after[2] - z), (after[1] - y) - up_y(x))


def curl_down(here, before):
    x, y, z = here
    return (down_y(z) - down_z(y), down_z(x) - (z - before[2]), (y - before[1]) - down_y(x))


def blur(block):
    table = kernel_table(RAD)
    lanes, count = block.shape[1], block.shape[0]
    sums = [block]
    for b in range(1, RAD + 1):
        sums.append(pltpu.roll(block, b, 1) + pltpu.roll(block, lanes - b, 1))
    total = None
    for a in range(RAD + 1):
        part = sum(float(table[RAD + a, RAD + b]) * sums[b] for b in range(RAD + 1))
        if a:
            part = pltpu.roll(part, a, 0) + pltpu.roll(part, count - a, 0)
        total = part if total is None else total + part
    return total


class Halos:
    def __init__(self, depth, x_sides, own, even, odd):
        self.depth = depth
        self.plan = Edges(depth)
        self.x_sides = x_sides
        self.own, self.even, self.odd = own, even, odd

    def of(self, row, at, count):
        if 0 <= row < 4:
            return self.own[at : at + count, :]
        side = self.x_sides.left if row < 0 else self.x_sides.right
        return self.x_sides.of(side, self.even, self.odd, at, count)

    def full(self, name, c, row):
        return unroll(self.of(row, 0, self.depth), self.plan.full_slot(name, c, row) * 2 * FULL_K)

    def window(self, name, c, row):
        at, slot = self.plan.window_slot(name, c, row)
        return unroll(self.of(row, self.plan.window_at + at, TILE), slot * 2 * WIN_K)


def unroll(block, shift):
    return pltpu.roll(block, LANES - shift, 1) if shift else block


class Coefficients:
    def __init__(self, region, densities):
        self.design = (region == 2.0).astype(jnp.float32)
        self.absorbing = (region == 1.0).astype(jnp.float32)
        self.source = (region == 3.0).astype(jnp.float32)
        self.inverse, self.slope = [], []
        for density in densities:
            inner = jnp.tanh(SHARP * (blur(density) - LEVEL))
            projected = (CREST + inner) / SCALE
            self.slope.append(SHARP * (1.0 - inner * inner) / SCALE)
            self.inverse.append(1.0 / (1.0 + CONTRAST * self.design * projected))
        damp = ABSORB * self.absorbing
        self.keep = (1.0 - damp) / (1.0 + damp)
        self.gain = COURANT / (1.0 + damp)


def inside_masks(x_sides, y_sides):
    lane = lane_index(TILE, 2 * LANES)
    inside = jnp.where(lane < LANES, 1.0, jnp.where(lane < LANES + LANES // 2, sum(y_sides.right), sum(y_sides.left)))
    return {"own": inside, "below": inside * sum(x_sides.left), "above": inside * sum(x_sides.right)}


def where_row(row):
    return "own" if 0 <= row < 4 else ("below" if row < 0 else "above")


def spread(block, row, count=TILE):
    at = row + DEN_BASE
    return jnp.broadcast_to(block[at : at + 1, :], (count, block.shape[1]))


def near_kernel(
    depth, columns, far, done_e, done_h, near,
    out_grad, out_e, out_h,
    grad, ratio_rows, sems,
):
    copies = [
        pltpu.make_async_copy(done_e, out_e, sems.at[0]),
        pltpu.make_async_copy(done_h, out_h, sems.at[1]),
        pltpu.make_async_copy(grad, out_grad, sems.at[2]),
    ]
    copies[0].start()
    copies[1].start()
    wide = 2 * LANES
    centre = depth // 2
    low = near_layers(depth)[0]

    def given(n, row):
        return [near[n, c, row + 3] for c in range(3)]

    odd = lax.rem(lax.axis_index("gx"), 2)
    far_at = jnp.where(odd == 1, DEN_BASE - 5, DEN_BASE + 8)
    at_far = lax.broadcasted_iota(jnp.int32, (16, wide), 0) == far_at
    densities = []
    for layer in range(2):
        row = jnp.concatenate([far[2 * layer : 2 * layer + 1, :], far[2 * layer + 1 : 2 * layer + 2, :]], 1)
        densities.append(jnp.where(at_far, jnp.broadcast_to(row, (16, wide)), columns[16 * layer : 16 * layer + 16, :]))
    known = Coefficients(columns[32:48, :], densities)
    inverse, slope, design, source = known.inverse, known.slope, known.design, known.source
    keep_col, gain_col = known.keep, known.gain
    masks = inside_masks(Sides("gx"), Sides("gy"))
    steps = {key: COURANT * value for key, value in masks.items()}

    sub = lax.broadcasted_iota(jnp.int32, (TILE, wide), 0) + low

    def layered(row):
        first, second = spread(inverse[0], row), spread(inverse[1], row)
        return jnp.where(sub == centre, first, jnp.where(sub == centre + 1, second, 1.0))

    keep_win = {row: spread(keep_col, row) for row in range(-3, 7)}
    layer_win = {row: layered(row) for row in range(-3, 7)}
    gain_win = {row: spread(gain_col, row) * layer_win[row] * masks[where_row(row)] for row in range(-3, 7)}
    source_plane = (sub == centre - 1).astype(jnp.float32)
    h1, e1, h2, drive1, drive2 = {}, {}, {}, {}, {}

    def minus_step(base, curl, row):
        step = steps[where_row(row)]
        return [b - step * c for b, c in zip(base, curl)]

    for row in range(-3, 7):
        h1[row], drive1[row] = given(0, row), given(1, row)
        e1[row] = [kept + gain_win[row] * d for kept, d in zip(given(2, row), drive1[row])]
    for row in range(-3, 6):
        h2[row] = minus_step(h1[row], curl_up(e1[row], e1[row + 1]), row)
    for row in range(-2, 6):
        drive2[row] = list(curl_down(h2[row], h2[row - 1]))
        drive2[row][2] = drive2[row][2] - math.sin(OMEGA * 2.0) * source_plane * spread(source, row)
    a2 = {row: given(3, row) for row in range(-3, 7)}
    ga_win = {row: [gain_win[row] * v for v in a2[row]] for row in range(-3, 7)}
    bh_win = {}
    for row in range(-3, 6):
        mask = masks[where_row(row)]
        curl = curl_up(ga_win[row], ga_win[row + 1])
        bh_win[row] = [v + mask * d for v, d in zip(given(4, row), curl)]
    ratio_rows[...] = jnp.zeros(ratio_rows.shape, jnp.float32)
    for row in range(-2, 6):
        a1 = minus_step(
            [keep_win[row] * v for v in a2[row]], curl_down(bh_win[row], bh_win[row - 1]), row
        )
        total = sum(a2[row][c] * drive2[row][c] + a1[c] * drive1[row][c] for c in range(3))
        for layer in range(2):
            at = centre + layer - low
            ratio_rows[layer, row + DEN_BASE : row + DEN_BASE + 1, :] = total[at : at + 1, :]
    for layer in range(2):
        sensitivity = -ratio_rows[layer] * gain_col * inverse[layer] * inverse[layer]
        smoothed = blur(CONTRAST * design * sensitivity * slope[layer])
        grad[layer] = smoothed[DEN_BASE : DEN_BASE + 4, :LANES]
    copies[2].start()
    for copy in copies:
        copy.wait()


def full_kernel(
    depth, e, h, ae, ah, from_even, from_odd, halo, halo_even, halo_odd, columns,
    out_e, out_h, near,
    ga, bh, be, gb,
):
    rows = Rows(depth, {"e": e, "h": h, "ae": ae, "ah": ah}, from_even, from_odd)
    halos = Halos(depth, rows.sides, halo, halo_even, halo_odd)
    wide = 2 * LANES
    centre = depth // 2

    def full(name, c, row):
        return jnp.concatenate([rows.full(name, c, row), halos.full(name, c, row)], 1)

    known = Coefficients(columns[32:48, :], [columns[16 * layer : 16 * layer + 16, :] for layer in range(2)])
    inverse, absorbing = known.inverse, known.absorbing
    masks = inside_masks(rows.sides, Sides("gy"))
    steps = {key: COURANT * value for key, value in masks.items()}

    def window(name, c, row):
        return jnp.concatenate([rows.window(name, c, row), halos.window(name, c, row)], 1)

    sub = lax.broadcasted_iota(jnp.int32, (TILE, wide), 0) + rows.low
    at_source = (sub == centre - 1).astype(jnp.float32) * math.sin(OMEGA)
    fields, magnetic = {}, {}
    for row in range(-4, 8):
        fields[row] = [window("e", c, row) for c in range(3)]
    for row in range(-4, 7):
        curl = curl_up(fields[row], fields[row + 1])
        magnetic[row] = [window("h", c, row) - steps[where_row(row)] * curl[c] for c in range(3)]
    for row in range(-3, 7):
        drive = list(curl_down(magnetic[row], magnetic[row - 1]))
        drive[2] = drive[2] - at_source * spread(known.source, row)
        keep = spread(known.keep, row)
        for c in range(3):
            near[0, c, row + 3] = magnetic[row][c]
            near[1, c, row + 3] = drive[c]
            near[2, c, row + 3] = keep * fields[row][c]
            near[3, c, row + 3] = window("ae", c, row)
            if row < 6:
                near[4, c, row + 3] = window("ah", c, row)

    z = lax.broadcasted_iota(jnp.int32, (depth, wide), 0)
    zf = z.astype(jnp.float32)
    margin = float(depth // 8)
    ramp = jnp.maximum(jnp.maximum((margin - zf) / margin, (zf - (depth - 1 - margin)) / margin), 0.0)
    open_damp = ABSORB * ramp * ramp
    full_damp = open_damp + ABSORB
    gain_open, gain_abs = COURANT / (1.0 + open_damp), COURANT / (1.0 + full_damp)
    keep_open, keep_abs = (1.0 - open_damp) / (1.0 + open_damp), (1.0 - full_damp) / (1.0 + full_damp)

    def coefficient(row):
        flag = spread(absorbing, row, depth) > 0.5
        layers = jnp.where(
            z == centre,
            spread(inverse[0], row, depth),
            jnp.where(z == centre + 1, spread(inverse[1], row, depth), 1.0),
        )
        return jnp.where(flag, keep_abs, keep_open), jnp.where(flag, gain_abs, gain_open) * layers

    def stretch(block):
        return jnp.broadcast_to(block[:1, :], (depth, wide))

    masks = {key: stretch(value) for key, value in masks.items()}
    steps = {key: stretch(value) for key, value in steps.items()}

    for row in range(-2, 6):
        keep, gain = coefficient(row)
        for c in range(3):
            value = full("ae", c, row)
            ga[c, row + 2] = gain * value
            if -1 <= row <= 4:
                be[c, row + 1] = keep * value
    for row in range(-2, 5):
        curl = curl_up([ga[c, row + 2] for c in range(3)], [ga[c, row + 3] for c in range(3)])
        for c in range(3):
            bh[c, row + 2] = full("ah", c, row) + masks[where_row(row)] * curl[c]
    for row in range(-1, 5):
        keep, gain = coefficient(row)
        curl = curl_down([bh[c, row + 2] for c in range(3)], [bh[c, row + 1] for c in range(3)])
        for c in range(3):
            value = be[c, row + 1] - steps[where_row(row)] * curl[c]
            be[c, row + 1] = keep * value
            gb[c, row + 1] = gain * value
    for row in range(-1, 4):
        curl = curl_up([gb[c, row + 1] for c in range(3)], [gb[c, row + 2] for c in range(3)])
        for c in range(3):
            value = bh[c, row + 2] + masks[where_row(row)] * curl[c]
            bh[c, row + 2] = value
            if row >= 0:
                out_h[c, row] = value[:, :LANES]
    for row in range(4):
        curl = curl_down([bh[c, row + 2] for c in range(3)], [bh[c, row + 1] for c in range(3)])
        for c in range(3):
            out_e[c, row] = be[c, row + 1][:, :LANES] - COURANT * curl[c][:, :LANES]


def per_device(density, e_field, h_field, adj_e, adj_h, region):
    depth = e_field.shape[2]
    sent, plan = Sent(depth), Edges(depth)
    f32 = jnp.float32
    params = pltpu.CompilerParams(vmem_limit_bytes=32 * 1024 * 1024)
    shape = jax.ShapeDtypeStruct
    near = e_field.shape[:2] + (2 * TILE, LANES)
    mate_den = pair_permute(density, x_even)
    own = pl.pallas_call(
        functools.partial(load_kernel, depth),
        out_shape=(
            pltpu.VMEM(density.shape, f32),
            pltpu.VMEM(near, f32),
            pltpu.VMEM(near, f32),
            pltpu.VMEM(adj_e.shape, f32),
            pltpu.VMEM(adj_h.shape, f32),
            pltpu.VMEM(region.shape, region.dtype),
        ),
        in_specs=[pl.BlockSpec(memory_space=pltpu.HBM)] * 6,
        scratch_shapes=[pltpu.SemaphoreType.DMA((6,))],
        compiler_params=pltpu.CompilerParams(vmem_limit_bytes=LOAD_VMEM),
        name="load",
    )(density, e_field, h_field, adj_e, adj_h, region)
    fields = own[1:5]
    edges, to_even, to_odd = pl.pallas_call(
        functools.partial(first_kernel, depth),
        out_shape=(
            shape((plan.rows, LANES), f32),
            shape((sent.rows, LANES), f32),
            shape((sent.rows, LANES), f32),
        ),
        compiler_params=params,
        name="first",
    )(*own, mate_den)
    edges_odd = pair_permute(edges, y_odd)
    edges_even = pair_permute(edges, y_even)
    from_odd = pair_permute(to_odd, x_odd)
    from_even = pair_permute(to_even, x_even)
    halo = pl.pallas_call(
        functools.partial(combine_kernel, depth),
        out_shape=shape((plan.rows, LANES), f32),
        compiler_params=params,
        name="combine",
    )(edges_even, edges_odd)
    halo_odd = pair_permute(halo, x_odd)
    halo_even = pair_permute(halo, x_even)
    wide = 2 * LANES
    columns, far = pl.pallas_call(
        functools.partial(columns_kernel, depth),
        out_shape=(shape((48, wide), f32), shape((TILE, LANES), f32)),
        compiler_params=params,
        name="columns",
    )(own[0], own[5], from_even, from_odd, halo, halo_even, halo_odd)
    far = pair_permute(far, x_even)
    done = pl.pallas_call(
        functools.partial(full_kernel, depth),
        out_shape=(
            pltpu.VMEM(e_field.shape, f32),
            pltpu.VMEM(e_field.shape, f32),
            pltpu.VMEM((5, 3, 10, TILE, wide), f32),
        ),
        scratch_shapes=[
            pltpu.VMEM((3, 8, depth, wide), f32),
            pltpu.VMEM((3, 7, depth, wide), f32),
            pltpu.VMEM((3, 6, depth, wide), f32),
            pltpu.VMEM((3, 6, depth, wide), f32),
        ],
        compiler_params=params,
        name="full",
    )(*fields, from_even, from_odd, halo, halo_even, halo_odd, columns)
    return pl.pallas_call(
        functools.partial(near_kernel, depth),
        out_shape=(shape(density.shape, f32), shape(e_field.shape, f32), shape(e_field.shape, f32)),
        out_specs=[pl.BlockSpec(memory_space=pltpu.HBM)] * 3,
        scratch_shapes=[
            pltpu.VMEM(density.shape, f32),
            pltpu.VMEM((2, 16, wide), f32),
            pltpu.SemaphoreType.DMA((3,)),
        ],
        compiler_params=params,
        name="near",
    )(columns, far, *done)


def solution(mesh):
    field = P(None, "gx", None, "gy")
    design = P(None, "gx", "gy")
    return jax.shard_map(
        per_device,
        mesh=mesh,
        in_specs=(design, field, field, field, field, P("gx", "gy")),
        out_specs=(design, field, field),
        check_vma=False,
    )
```

```python
import functools
import math

import jax
import jax.numpy as jnp
import numpy as np
from jax import lax
from jax.experimental import pallas as pl
from jax.experimental.pallas import tpu as pltpu
from jax.sharding import PartitionSpec as P

RAD = 2
COURANT = 0.5
SHARP = 4.0
LEVEL = 0.5
CONTRAST = 5.0
ABSORB = 0.3
OMEGA = 0.7
CREST = math.tanh(SHARP * LEVEL)
SCALE = CREST + math.tanh(SHARP * (1.0 - LEVEL))

LANES = 128
LOAD_VMEM = 56 * 1024 * 1024
TILE = 8
FULL_K = 2
WIN_K = 4
FIRST, LAST = -4, 8
DEN_BASE = 6


def kernel_table(radius):
    offsets = np.arange(-radius, radius + 1)
    distance = np.sqrt(offsets[:, None] ** 2 + offsets[None, :] ** 2)
    table = np.maximum(0.0, radius + 1.0 - distance)
    return table / table.sum()


def odd_swap(index):
    return ((index + 1) ^ 1) - 1


def pair_permute(block, partner):
    count_x, count_y = lax.axis_size("gx"), lax.axis_size("gy")
    route = []
    for i in range(count_x):
        for j in range(count_y):
            a, b = partner(i, j, count_x, count_y)
            route.append((i * count_y + j, a * count_y + b))
    return lax.ppermute(block, ("gx", "gy"), route)


def x_even(i, j, nx, ny):
    return i ^ 1, j


def x_odd(i, j, nx, ny):
    return (odd_swap(i), j) if 0 < i < nx - 1 else (i, j ^ 1)


def x_ring(i, j, nx, ny):
    if 0 < i < nx - 1:
        return odd_swap(i), j
    return (i, odd_swap(j)) if 0 < j < ny - 1 else (nx - 1 - i, j)


def y_even(i, j, nx, ny):
    return i, j ^ 1


def y_odd(i, j, nx, ny):
    return (i, odd_swap(j)) if 0 < j < ny - 1 else (i ^ 1, j)


PIECES = (
    ("e", 1, (0, 1, 2), 6, -2, -2),
    ("e", 2, (0, 1, 2), 6, -2, -2),
    ("e", 3, (0, 1, 2), 5, -1, -2),
    ("e", 4, (0, 1, 2), 4, 0, -2),
    ("h", 1, (0, 1, 2), 5, -2, -2),
    ("h", 2, (0, 1, 2), 5, -2, -2),
    ("h", 3, (0, 1, 2), 4, -1, -2),
    ("h", 4, (1, 2), 3, 0, 0),
    ("ae", 3, (0, 1, 2), 3, 0, -1),
    ("ah", 3, (1, 2), 2, 0, 0),
    ("ah", 2, (0,), 3, -1, -1),
)


class Sent:
    def __init__(self, depth):
        self.full = {}
        at = 0
        for name, far in (("ae", (0, 1, 2)), ("ah", (1, 2))):
            for distance in (1, 2):
                for c in (0, 1, 2) if distance == 1 else far:
                    self.full[name, c, distance] = at
                    at += depth
        self.pieces = {}
        for name, distance, components, count, left, right in PIECES:
            for c in components:
                self.pieces[name, c, distance] = at, count, left, right
                at += count
        at = -(-at // TILE) * TILE
        self.density = at
        self.region = at + TILE
        self.mate = at + 2 * TILE
        self.rows = at + 3 * TILE


FIELDS = ("ae", "ah", "e", "h")


COLUMN_K = 8
COLUMN_LANE = 104


class Edges:
    def __init__(self, depth):
        self.window_at = depth
        self.rows = depth + 3 * TILE
        self.density, self.region, self.mate = 0, TILE, 2 * TILE

    def full_slot(self, name, c, row):
        return row % 4 * 6 + FIELDS.index(name) * 3 + c

    def window_slot(self, name, c, row):
        place = (FIELDS.index(name) * 3 + c) * 4 + row % 4
        return place // 16 * TILE, place % 16


def lane_index(rows, lanes=LANES):
    return lax.broadcasted_iota(jnp.int32, (rows, lanes), 1)


def pack(planes, width):
    slots = LANES // (2 * width)
    owner = lax.rem((lane_index(planes[0].shape[0]) + width) // (2 * width), slots)
    total = None
    for slot, plane in enumerate(planes):
        moved = pltpu.roll(plane, slot * 2 * width, 1) if slot else plane
        total = moved if total is None else jnp.where(owner == slot, moved, total)
    return total


def near_layers(depth):
    low = depth // 2 - 4
    return low, low // TILE * TILE


def load_kernel(depth, den, e, h, ae, ah, reg, own_den, own_e, own_h, own_ae, own_ah, own_reg, sems):
    near = pl.ds(near_layers(depth)[1], 2 * TILE)
    pairs = (
        (ae, own_ae),
        (ah, own_ah),
        (e.at[:, :, near, :], own_e),
        (h.at[:, :, near, :], own_h),
        (den, own_den),
        (reg, own_reg),
    )
    copies = [pltpu.make_async_copy(source, target, sems.at[n]) for n, (source, target) in enumerate(pairs)]
    for copy in copies:
        copy.start()
    for copy in copies:
        copy.wait()


def near_windows(depth, e, h, ae, ah):
    low, base = near_layers(depth)
    windows = []
    for field, start in ((ae, low), (ah, low), (e, low - base), (h, low - base)):
        for c in range(3):
            for row in range(4):
                windows.append(field[c, row, start : start + TILE, :])
    return windows


def first_kernel(depth, den, e, h, ae, ah, reg, mate_den, edges, to_even, to_odd):
    plan, sent = Edges(depth), Sent(depth)
    low = near_layers(depth)[0]
    odd = lax.rem(lax.axis_index("gx"), 2)
    own = {"ae": ae, "ah": ah}
    windows = near_windows(depth, e, h, ae, ah)
    centre = depth // 2
    base = near_layers(depth)[1]
    fields = {"ae": (ae, centre), "ah": (ah, centre), "e": (e, centre - base), "h": (h, centre - base)}
    for ref, right in ((to_even, 1 - odd), (to_odd, odd)):
        row_of = lambda distance: right * (ae.shape[1] + 1 - 2 * distance) + distance - 1
        for (name, c, distance), at in sent.full.items():
            ref[at : at + depth, :] = own[name][c, row_of(distance)]
        for (name, c, distance), (at, count, from_left, from_right) in sent.pieces.items():
            field, middle = fields[name]
            row = row_of(distance)
            value = field[c, row, middle + from_left : middle + from_left + count, :]
            if from_left != from_right:
                other = field[c, row, middle + from_right : middle + from_right + count, :]
                value = jnp.where(jnp.full(value.shape, right, jnp.int32) == 1, value, other)
            ref[at : at + count, :] = value
    planes = [own[name][c, row] for row in range(4) for name in ("ae", "ah") for c in range(3)]
    blank = jnp.zeros((4, LANES), jnp.float32)
    column = jnp.concatenate(
        [den[0], den[1], reg[...].astype(jnp.float32), blank, mate_den[0], mate_den[1]]
        + [blank] * ((depth - 3 * TILE) // 4),
        0,
    )
    lane = lane_index(depth)
    mine = (lane >= COLUMN_LANE - COLUMN_K) & (lane < COLUMN_LANE + COLUMN_K)
    edges[0:depth, :] = jnp.where(mine, pltpu.roll(column, COLUMN_LANE, 1), pack(planes, FULL_K))
    for n in range(3):
        at = plan.window_at + n * TILE
        edges[at : at + TILE, :] = pack(windows[16 * n : 16 * n + 16], WIN_K)
    for ref in (to_even, to_odd):
        at = sent.density
        ref[at : at + 3 * TILE, :] = column[: 3 * TILE]


def as_float(flag):
    return flag.astype(jnp.float32)


class Sides:
    def __init__(self, axis):
        index = lax.axis_index(axis)
        last = lax.axis_size(axis) - 1
        odd = lax.rem(index, 2)
        even = 1 - odd
        self.left = as_float(odd), as_float(even * (index > 0).astype(jnp.int32))
        self.right = as_float(even), as_float(odd * (index < last).astype(jnp.int32))

    @staticmethod
    def of(side, even, odd, at, count):
        return side[0] * even[at : at + count, :] + side[1] * odd[at : at + count, :]


class Rows:
    def __init__(self, depth, own, from_even, from_odd):
        self.sides = Sides("gx")
        self.sent = Sent(depth)
        self.depth = depth
        self.low, self.base = near_layers(depth)
        self.own = own
        self.even, self.odd = from_even, from_odd

    def of(self, row, at, count):
        side = self.sides.left if row < 0 else self.sides.right
        return self.sides.of(side, self.even, self.odd, at, count)

    def full(self, name, c, row):
        if 0 <= row < 4:
            return self.own[name][c, row]
        distance = -row if row < 0 else row - 3
        if (name, c, distance) not in self.sent.full:
            return jnp.zeros((self.depth, LANES), jnp.float32)
        return self.of(row, self.sent.full[name, c, distance], self.depth)

    def window(self, name, c, row):
        sent = self.sent
        if 0 <= row < 4:
            low = self.low - self.base if name in ("e", "h") else self.low
            return self.own[name][c, row, low : low + TILE, :]
        distance = -row if row < 0 else row - 3
        if (name, c, distance) in sent.full:
            return self.of(row, sent.full[name, c, distance] + self.low, TILE)
        if (name, c, distance) not in sent.pieces:
            return jnp.zeros((TILE, LANES), jnp.float32)
        at, count, from_left, from_right = sent.pieces[name, c, distance]
        at -= self.depth // 2 - self.low + (from_left if row < 0 else from_right)
        return self.of(row, at, TILE)


def combine_kernel(depth, odd, even, halo):
    plan = Edges(depth)
    sides = Sides("gy")
    for at, end, width in ((0, plan.window_at, FULL_K), (plan.window_at, plan.rows, WIN_K)):
        lane = lane_index(end - at)
        from_left = lax.rem(lane, 2 * width) >= width
        if at == 0:
            beside = (lane >= COLUMN_LANE - COLUMN_K) & (lane < COLUMN_LANE + COLUMN_K)
            from_left = jnp.where(beside, (lane < COLUMN_LANE).astype(jnp.int32), from_left.astype(jnp.int32)) == 1
        left = sides.of(sides.left, even, odd, at, end - at)
        right = sides.of(sides.right, even, odd, at, end - at)
        halo[at:end, :] = jnp.where(from_left, left, right)


def columns_kernel(depth, den, reg, from_odd, from_even, halo, halo_even, halo_odd, columns, far):
    sent = Sent(depth)
    sides = Sides("gx")
    odd = as_float(lax.rem(lax.axis_index("gx"), 2))
    count = 3 * TILE

    def beside(ref):
        return pltpu.roll(ref[0:count, :], LANES - COLUMN_LANE, 1)

    def within(ref):
        return ref[sent.density : sent.density + count, :]

    for lane, (own, even, away) in enumerate(
        ((None, within(from_even), within(from_odd)), (beside(halo), beside(halo_even), beside(halo_odd)))
    ):
        lanes = pl.ds(lane * LANES, LANES)
        below = sides.left[0] * even + sides.left[1] * away
        above = sides.right[0] * even + sides.right[1] * away
        zero_row = jnp.zeros((1, LANES), jnp.float32)
        mate = 2 * TILE
        for n in range(3):
            if own is None:
                here = den[n] if n < 2 else reg[...].astype(jnp.float32)
            else:
                here = own[4 * n : 4 * n + 4]
            to = 16 * n
            columns[to : to + 1, lanes] = zero_row
            columns[to + 15 : to + 16, lanes] = zero_row
            first = last = zero_row
            if n < 2:
                first = sides.left[1] * away[mate + 4 * n + 3 : mate + 4 * n + 4]
                last = sides.right[1] * away[mate + 4 * n : mate + 4 * n + 1]
                far[2 * n + lane : 2 * n + lane + 1, :] = (1.0 - odd) * below[4 * n + 3 : 4 * n + 4] + odd * above[4 * n : 4 * n + 1]
            columns[to + 1 : to + 2, lanes] = first
            columns[to + 2 : to + 6, lanes] = below[4 * n : 4 * n + 4]
            columns[to + 6 : to + 10, lanes] = here
            columns[to + 10 : to + 14, lanes] = above[4 * n : 4 * n + 4]
            columns[to + 14 : to + 15, lanes] = last
    far[4:8, :] = jnp.zeros((4, LANES), jnp.float32)


def up_z(block):
    depth = block.shape[0]
    moved = pltpu.roll(block, depth - 1, 0)
    if depth == TILE:
        return moved - block
    edge = lax.broadcasted_iota(jnp.int32, block.shape, 0) == depth - 1
    return jnp.where(edge, 0.0, moved) - block


def down_z(block):
    moved = pltpu.roll(block, 1, 0)
    if block.shape[0] == TILE:
        return block - moved
    edge = lax.broadcasted_iota(jnp.int32, block.shape, 0) == 0
    return block - jnp.where(edge, 0.0, moved)


def up_y(block):
    return pltpu.roll(block, block.shape[1] - 1, 1) - block


def down_y(block):
    return block - pltpu.roll(block, 1, 1)


def curl_up(here, after):
    x, y, z = here
    return (up_y(z) - up_z(y), up_z(x) - (after[2] - z), (after[1] - y) - up_y(x))


def curl_down(here, before):
    x, y, z = here
    return (down_y(z) - down_z(y), down_z(x) - (z - before[2]), (y - before[1]) - down_y(x))


def blur(block):
    table = kernel_table(RAD)
    lanes, count = block.shape[1], block.shape[0]
    sums = [block]
    for b in range(1, RAD + 1):
        sums.append(pltpu.roll(block, b, 1) + pltpu.roll(block, lanes - b, 1))
    total = None
    for a in range(RAD + 1):
        part = sum(float(table[RAD + a, RAD + b]) * sums[b] for b in range(RAD + 1))
        if a:
            part = pltpu.roll(part, a, 0) + pltpu.roll(part, count - a, 0)
        total = part if total is None else total + part
    return total


class Halos:
    def __init__(self, depth, x_sides, own, even, odd):
        self.depth = depth
        self.plan = Edges(depth)
        self.x_sides = x_sides
        self.own, self.even, self.odd = own, even, odd

    def of(self, row, at, count):
        if 0 <= row < 4:
            return self.own[at : at + count, :]
        side = self.x_sides.left if row < 0 else self.x_sides.right
        return self.x_sides.of(side, self.even, self.odd, at, count)

    def full(self, name, c, row):
        return unroll(self.of(row, 0, self.depth), self.plan.full_slot(name, c, row) * 2 * FULL_K)

    def window(self, name, c, row):
        at, slot = self.plan.window_slot(name, c, row)
        return unroll(self.of(row, self.plan.window_at + at, TILE), slot * 2 * WIN_K)


def unroll(block, shift):
    return pltpu.roll(block, LANES - shift, 1) if shift else block


class Coefficients:
    def __init__(self, region, densities):
        self.design = (region == 2.0).astype(jnp.float32)
        self.absorbing = (region == 1.0).astype(jnp.float32)
        self.source = (region == 3.0).astype(jnp.float32)
        self.inverse, self.slope = [], []
        for density in densities:
            inner = jnp.tanh(SHARP * (blur(density) - LEVEL))
            projected = (CREST + inner) / SCALE
            self.slope.append(SHARP * (1.0 - inner * inner) / SCALE)
            self.inverse.append(1.0 / (1.0 + CONTRAST * self.design * projected))
        damp = ABSORB * self.absorbing
        self.keep = (1.0 - damp) / (1.0 + damp)
        self.gain = COURANT / (1.0 + damp)


def inside_masks(x_sides, y_sides):
    lane = lane_index(TILE, 2 * LANES)
    inside = jnp.where(lane < LANES, 1.0, jnp.where(lane < LANES + LANES // 2, sum(y_sides.right), sum(y_sides.left)))
    return {"own": inside, "below": inside * sum(x_sides.left), "above": inside * sum(x_sides.right)}


def where_row(row):
    return "own" if 0 <= row < 4 else ("below" if row < 0 else "above")


def spread(block, row, count=TILE):
    at = row + DEN_BASE
    return jnp.broadcast_to(block[at : at + 1, :], (count, block.shape[1]))


def near_kernel(
    depth, columns, far, done_e, done_h, near,
    out_grad, out_e, out_h,
    grad, ratio_rows, sems,
):
    copies = [
        pltpu.make_async_copy(done_e, out_e, sems.at[0]),
        pltpu.make_async_copy(done_h, out_h, sems.at[1]),
        pltpu.make_async_copy(grad, out_grad, sems.at[2]),
    ]
    copies[0].start()
    copies[1].start()
    wide = 2 * LANES
    centre = depth // 2
    low = near_layers(depth)[0]

    def given(n, row):
        return [near[n, c, row + 3] for c in range(3)]

    odd = lax.rem(lax.axis_index("gx"), 2)
    far_at = jnp.where(odd == 1, DEN_BASE - 5, DEN_BASE + 8)
    at_far = lax.broadcasted_iota(jnp.int32, (16, wide), 0) == far_at
    densities = []
    for layer in range(2):
        row = jnp.concatenate([far[2 * layer : 2 * layer + 1, :], far[2 * layer + 1 : 2 * layer + 2, :]], 1)
        densities.append(jnp.where(at_far, jnp.broadcast_to(row, (16, wide)), columns[16 * layer : 16 * layer + 16, :]))
    known = Coefficients(columns[32:48, :], densities)
    inverse, slope, design, source = known.inverse, known.slope, known.design, known.source
    keep_col, gain_col = known.keep, known.gain
    masks = inside_masks(Sides("gx"), Sides("gy"))
    steps = {key: COURANT * value for key, value in masks.items()}

    sub = lax.broadcasted_iota(jnp.int32, (TILE, wide), 0) + low

    def layered(row):
        first, second = spread(inverse[0], row), spread(inverse[1], row)
        return jnp.where(sub == centre, first, jnp.where(sub == centre + 1, second, 1.0))

    keep_win = {row: spread(keep_col, row) for row in range(-3, 7)}
    layer_win = {row: layered(row) for row in range(-3, 7)}
    gain_win = {row: spread(gain_col, row) * layer_win[row] * masks[where_row(row)] for row in range(-3, 7)}
    source_plane = (sub == centre - 1).astype(jnp.float32)
    h1, e1, h2, drive1, drive2 = {}, {}, {}, {}, {}

    def minus_step(base, curl, row):
        step = steps[where_row(row)]
        return [b - step * c for b, c in zip(base, curl)]

    for row in range(-3, 7):
        h1[row], drive1[row] = given(0, row), given(1, row)
        e1[row] = [kept + gain_win[row] * d for kept, d in zip(given(2, row), drive1[row])]
    for row in range(-3, 6):
        h2[row] = minus_step(h1[row], curl_up(e1[row], e1[row + 1]), row)
    for row in range(-2, 6):
        drive2[row] = list(curl_down(h2[row], h2[row - 1]))
        drive2[row][2] = drive2[row][2] - math.sin(OMEGA * 2.0) * source_plane * spread(source, row)
    a2 = {row: given(3, row) for row in range(-3, 7)}
    ga_win = {row: [gain_win[row] * v for v in a2[row]] for row in range(-3, 7)}
    bh_win = {}
    for row in range(-3, 6):
        mask = masks[where_row(row)]
        curl = curl_up(ga_win[row], ga_win[row + 1])
        bh_win[row] = [v + mask * d for v, d in zip(given(4, row), curl)]
    ratio_rows[...] = jnp.zeros(ratio_rows.shape, jnp.float32)
    for row in range(-2, 6):
        a1 = minus_step(
            [keep_win[row] * v for v in a2[row]], curl_down(bh_win[row], bh_win[row - 1]), row
        )
        total = sum(a2[row][c] * drive2[row][c] + a1[c] * drive1[row][c] for c in range(3))
        for layer in range(2):
            at = centre + layer - low
            ratio_rows[layer, row + DEN_BASE : row + DEN_BASE + 1, :] = total[at : at + 1, :]
    for layer in range(2):
        sensitivity = -ratio_rows[layer] * gain_col * inverse[layer] * inverse[layer]
        smoothed = blur(CONTRAST * design * sensitivity * slope[layer])
        grad[layer] = smoothed[DEN_BASE : DEN_BASE + 4, :LANES]
    copies[2].start()
    for copy in copies:
        copy.wait()


def full_kernel(
    depth, e, h, ae, ah, from_even, from_odd, halo, halo_even, halo_odd, columns,
    out_e, out_h, near,
    ga, bh, be, gb,
):
    rows = Rows(depth, {"e": e, "h": h, "ae": ae, "ah": ah}, from_even, from_odd)
    halos = Halos(depth, rows.sides, halo, halo_even, halo_odd)
    wide = 2 * LANES
    centre = depth // 2

    def full(name, c, row):
        return jnp.concatenate([rows.full(name, c, row), halos.full(name, c, row)], 1)

    known = Coefficients(columns[32:48, :], [columns[16 * layer : 16 * layer + 16, :] for layer in range(2)])
    inverse, absorbing = known.inverse, known.absorbing
    masks = inside_masks(rows.sides, Sides("gy"))
    steps = {key: COURANT * value for key, value in masks.items()}

    def window(name, c, row):
        return jnp.concatenate([rows.window(name, c, row), halos.window(name, c, row)], 1)

    sub = lax.broadcasted_iota(jnp.int32, (TILE, wide), 0) + rows.low
    at_source = (sub == centre - 1).astype(jnp.float32) * math.sin(OMEGA)
    fields, magnetic = {}, {}
    for row in range(-4, 8):
        fields[row] = [window("e", c, row) for c in range(3)]
    for row in range(-4, 7):
        curl = curl_up(fields[row], fields[row + 1])
        magnetic[row] = [window("h", c, row) - steps[where_row(row)] * curl[c] for c in range(3)]
    for row in range(-3, 7):
        drive = list(curl_down(magnetic[row], magnetic[row - 1]))
        drive[2] = drive[2] - at_source * spread(known.source, row)
        keep = spread(known.keep, row)
        for c in range(3):
            near[0, c, row + 3] = magnetic[row][c]
            near[1, c, row + 3] = drive[c]
            near[2, c, row + 3] = keep * fields[row][c]
            near[3, c, row + 3] = window("ae", c, row)
            if row < 6:
                near[4, c, row + 3] = window("ah", c, row)

    z = lax.broadcasted_iota(jnp.int32, (depth, wide), 0)
    zf = z.astype(jnp.float32)
    margin = float(depth // 8)
    ramp = jnp.maximum(jnp.maximum((margin - zf) / margin, (zf - (depth - 1 - margin)) / margin), 0.0)
    open_damp = ABSORB * ramp * ramp
    full_damp = open_damp + ABSORB
    gain_open, gain_abs = COURANT / (1.0 + open_damp), COURANT / (1.0 + full_damp)
    keep_open, keep_abs = (1.0 - open_damp) / (1.0 + open_damp), (1.0 - full_damp) / (1.0 + full_damp)

    def coefficient(row):
        flag = spread(absorbing, row, depth) > 0.5
        layers = jnp.where(
            z == centre,
            spread(inverse[0], row, depth),
            jnp.where(z == centre + 1, spread(inverse[1], row, depth), 1.0),
        )
        return jnp.where(flag, keep_abs, keep_open), jnp.where(flag, gain_abs, gain_open) * layers

    def stretch(block):
        return jnp.broadcast_to(block[:1, :], (depth, wide))

    masks = {key: stretch(value) for key, value in masks.items()}
    steps = {key: stretch(value) for key, value in steps.items()}

    for row in range(-2, 6):
        keep, gain = coefficient(row)
        for c in range(3):
            value = full("ae", c, row)
            ga[c, row + 2] = gain * value
            if -1 <= row <= 4:
                be[c, row + 1] = keep * value
    for row in range(-2, 5):
        curl = curl_up([ga[c, row + 2] for c in range(3)], [ga[c, row + 3] for c in range(3)])
        for c in range(3):
            bh[c, row + 2] = full("ah", c, row) + masks[where_row(row)] * curl[c]
    for row in range(-1, 5):
        keep, gain = coefficient(row)
        curl = curl_down([bh[c, row + 2] for c in range(3)], [bh[c, row + 1] for c in range(3)])
        for c in range(3):
            value = be[c, row + 1] - steps[where_row(row)] * curl[c]
            be[c, row + 1] = keep * value
            gb[c, row + 1] = gain * value
    for row in range(-1, 4):
        curl = curl_up([gb[c, row + 1] for c in range(3)], [gb[c, row + 2] for c in range(3)])
        for c in range(3):
            value = bh[c, row + 2] + masks[where_row(row)] * curl[c]
            bh[c, row + 2] = value
            if row >= 0:
                out_h[c, row] = value[:, :LANES]
    for row in range(4):
        curl = curl_down([bh[c, row + 2] for c in range(3)], [bh[c, row + 1] for c in range(3)])
        for c in range(3):
            out_e[c, row] = be[c, row + 1][:, :LANES] - COURANT * curl[c][:, :LANES]


def per_device(density, e_field, h_field, adj_e, adj_h, region):
    depth = e_field.shape[2]
    sent, plan = Sent(depth), Edges(depth)
    f32 = jnp.float32
    params = pltpu.CompilerParams(vmem_limit_bytes=32 * 1024 * 1024)
    shape = jax.ShapeDtypeStruct
    near = e_field.shape[:2] + (2 * TILE, LANES)
    mate_den = pair_permute(density, x_even)
    own = pl.pallas_call(
        functools.partial(load_kernel, depth),
        out_shape=(
            pltpu.VMEM(density.shape, f32),
            pltpu.VMEM(near, f32),
            pltpu.VMEM(near, f32),
            pltpu.VMEM(adj_e.shape, f32),
            pltpu.VMEM(adj_h.shape, f32),
            pltpu.VMEM(region.shape, region.dtype),
        ),
        in_specs=[pl.BlockSpec(memory_space=pltpu.HBM)] * 6,
        scratch_shapes=[pltpu.SemaphoreType.DMA((6,))],
        compiler_params=pltpu.CompilerParams(vmem_limit_bytes=LOAD_VMEM),
        name="load",
    )(density, e_field, h_field, adj_e, adj_h, region)
    fields = own[1:5]
    edges, to_even, to_odd = pl.pallas_call(
        functools.partial(first_kernel, depth),
        out_shape=(
            shape((plan.rows, LANES), f32),
            shape((sent.rows, LANES), f32),
            shape((sent.rows, LANES), f32),
        ),
        compiler_params=params,
        name="first",
    )(*own, mate_den)
    edges_even = pair_permute(edges, y_even)
    edges_odd = pair_permute(edges, y_odd)
    from_odd = pair_permute(to_odd, x_odd)
    from_even = pair_permute(to_even, x_even)
    halo = pl.pallas_call(
        functools.partial(combine_kernel, depth),
        out_shape=shape((plan.rows, LANES), f32),
        compiler_params=params,
        name="combine",
    )(edges_odd, edges_even)
    halo_odd = pair_permute(halo, x_odd)
    halo_even = pair_permute(halo, x_even)
    wide = 2 * LANES
    columns, far = pl.pallas_call(
        functools.partial(columns_kernel, depth),
        out_shape=(shape((48, wide), f32), shape((TILE, LANES), f32)),
        compiler_params=params,
        name="columns",
    )(own[0], own[5], from_odd, from_even, halo, halo_even, halo_odd)
    far = pair_permute(far, x_even)
    done = pl.pallas_call(
        functools.partial(full_kernel, depth),
        out_shape=(
            pltpu.VMEM(e_field.shape, f32),
            pltpu.VMEM(e_field.shape, f32),
            pltpu.VMEM((5, 3, 10, TILE, wide), f32),
        ),
        scratch_shapes=[
            pltpu.VMEM((3, 8, depth, wide), f32),
            pltpu.VMEM((3, 7, depth, wide), f32),
            pltpu.VMEM((3, 6, depth, wide), f32),
            pltpu.VMEM((3, 6, depth, wide), f32),
        ],
        compiler_params=params,
        name="full",
    )(*fields, from_even, from_odd, halo, halo_even, halo_odd, columns)
    return pl.pallas_call(
        functools.partial(near_kernel, depth),
        out_shape=(shape(density.shape, f32), shape(e_field.shape, f32), shape(e_field.shape, f32)),
        out_specs=[pl.BlockSpec(memory_space=pltpu.HBM)] * 3,
        scratch_shapes=[
            pltpu.VMEM(density.shape, f32),
            pltpu.VMEM((2, 16, wide), f32),
            pltpu.SemaphoreType.DMA((3,)),
        ],
        compiler_params=params,
        name="near",
    )(columns, far, *done)


def solution(mesh):
    field = P(None, "gx", None, "gy")
    design = P(None, "gx", "gy")
    return jax.shard_map(
        per_device,
        mesh=mesh,
        in_specs=(design, field, field, field, field, P("gx", "gy")),
        out_specs=(design, field, field),
        check_vma=False,
    )
```

```python
import functools
import math

import jax
import jax.numpy as jnp
import numpy as np
from jax import lax
from jax.experimental import pallas as pl
from jax.experimental.pallas import tpu as pltpu
from jax.sharding import PartitionSpec as P

RAD = 2
COURANT = 0.5
SHARP = 4.0
LEVEL = 0.5
CONTRAST = 5.0
ABSORB = 0.3
OMEGA = 0.7
CREST = math.tanh(SHARP * LEVEL)
SCALE = CREST + math.tanh(SHARP * (1.0 - LEVEL))

LANES = 128
LOAD_VMEM = 56 * 1024 * 1024
TILE = 8
FULL_K = 2
WIN_K = 4
FIRST, LAST = -4, 8
DEN_BASE = 6


def kernel_table(radius):
    offsets = np.arange(-radius, radius + 1)
    distance = np.sqrt(offsets[:, None] ** 2 + offsets[None, :] ** 2)
    table = np.maximum(0.0, radius + 1.0 - distance)
    return table / table.sum()


def odd_swap(index):
    return ((index + 1) ^ 1) - 1


def pair_permute(block, partner):
    count_x, count_y = lax.axis_size("gx"), lax.axis_size("gy")
    route = []
    for i in range(count_x):
        for j in range(count_y):
            a, b = partner(i, j, count_x, count_y)
            route.append((i * count_y + j, a * count_y + b))
    return lax.ppermute(block, ("gx", "gy"), route)


def x_even(i, j, nx, ny):
    return i ^ 1, j


def x_odd(i, j, nx, ny):
    return (odd_swap(i), j) if 0 < i < nx - 1 else (i, j ^ 1)


def x_ring(i, j, nx, ny):
    if 0 < i < nx - 1:
        return odd_swap(i), j
    if i == 0:
        return (0, j - 1) if j > 0 else (nx - 1, j)
    return (i, j + 1) if j < ny - 1 else (0, j)


def y_even(i, j, nx, ny):
    return i, j ^ 1


def y_odd(i, j, nx, ny):
    return (i, odd_swap(j)) if 0 < j < ny - 1 else (i ^ 1, j)


PIECES = (
    ("e", 1, (0, 1, 2), 6, -2, -2),
    ("e", 2, (0, 1, 2), 6, -2, -2),
    ("e", 3, (0, 1, 2), 5, -1, -2),
    ("e", 4, (0, 1, 2), 4, 0, -2),
    ("h", 1, (0, 1, 2), 5, -2, -2),
    ("h", 2, (0, 1, 2), 5, -2, -2),
    ("h", 3, (0, 1, 2), 4, -1, -2),
    ("h", 4, (1, 2), 3, 0, 0),
    ("ae", 3, (0, 1, 2), 3, 0, -1),
    ("ah", 3, (1, 2), 2, 0, 0),
    ("ah", 2, (0,), 3, -1, -1),
)


class Sent:
    def __init__(self, depth):
        self.full = {}
        at = 0
        for name, far in (("ae", (0, 1, 2)), ("ah", (1, 2))):
            for distance in (1, 2):
                for c in (0, 1, 2) if distance == 1 else far:
                    self.full[name, c, distance] = at
                    at += depth
        self.pieces = {}
        for name, distance, components, count, left, right in PIECES:
            for c in components:
                self.pieces[name, c, distance] = at, count, left, right
                at += count
        at = -(-at // TILE) * TILE
        self.density = at
        self.region = at + TILE
        self.mate = at + 2 * TILE
        self.rows = at + 3 * TILE


FIELDS = ("ae", "ah", "e", "h")


COLUMN_K = 8
COLUMN_LANE = 104


class Edges:
    def __init__(self, depth):
        self.window_at = depth
        self.rows = depth + 3 * TILE
        self.density, self.region, self.mate = 0, TILE, 2 * TILE

    def full_slot(self, name, c, row):
        return row % 4 * 6 + FIELDS.index(name) * 3 + c

    def window_slot(self, name, c, row):
        place = (FIELDS.index(name) * 3 + c) * 4 + row % 4
        return place // 16 * TILE, place % 16


def lane_index(rows, lanes=LANES):
    return lax.broadcasted_iota(jnp.int32, (rows, lanes), 1)


def pack(planes, width):
    slots = LANES // (2 * width)
    owner = lax.rem((lane_index(planes[0].shape[0]) + width) // (2 * width), slots)
    total = None
    for slot, plane in enumerate(planes):
        moved = pltpu.roll(plane, slot * 2 * width, 1) if slot else plane
        total = moved if total is None else jnp.where(owner == slot, moved, total)
    return total


def near_layers(depth):
    low = depth // 2 - 4
    return low, low // TILE * TILE


def load_kernel(depth, den, e, h, ae, ah, reg, own_den, own_e, own_h, own_ae, own_ah, own_reg, packed, sems):
    near = pl.ds(near_layers(depth)[1], 2 * TILE)
    pairs = (
        (ae, own_ae),
        (ah, own_ah),
        (e.at[:, :, near, :], own_e),
        (h.at[:, :, near, :], own_h),
        (den, own_den),
        (reg, own_reg),
    )
    copies = [pltpu.make_async_copy(source, target, sems.at[n]) for n, (source, target) in enumerate(pairs)]
    for copy in copies:
        copy.start()
    copies[0].wait()
    copies[1].wait()
    own = (own_ae, own_ah)
    packed[...] = pack([field[c, row] for row in range(4) for field in own for c in range(3)], FULL_K)
    for copy in copies[2:]:
        copy.wait()


def near_windows(depth, e, h, ae, ah):
    low, base = near_layers(depth)
    windows = []
    for field, start in ((ae, low), (ah, low), (e, low - base), (h, low - base)):
        for c in range(3):
            for row in range(4):
                windows.append(field[c, row, start : start + TILE, :])
    return windows


def first_kernel(depth, den, e, h, ae, ah, reg, packed, mate_den, edges, to_even, to_odd):
    plan, sent = Edges(depth), Sent(depth)
    low = near_layers(depth)[0]
    odd = lax.rem(lax.axis_index("gx"), 2)
    own = {"ae": ae, "ah": ah}
    windows = near_windows(depth, e, h, ae, ah)
    centre = depth // 2
    base = near_layers(depth)[1]
    fields = {"ae": (ae, centre), "ah": (ah, centre), "e": (e, centre - base), "h": (h, centre - base)}
    for ref, right in ((to_even, 1 - odd), (to_odd, odd)):
        row_of = lambda distance: right * (ae.shape[1] + 1 - 2 * distance) + distance - 1
        for (name, c, distance), at in sent.full.items():
            ref[at : at + depth, :] = own[name][c, row_of(distance)]
        for (name, c, distance), (at, count, from_left, from_right) in sent.pieces.items():
            field, middle = fields[name]
            row = row_of(distance)
            value = field[c, row, middle + from_left : middle + from_left + count, :]
            if from_left != from_right:
                other = field[c, row, middle + from_right : middle + from_right + count, :]
                value = jnp.where(jnp.full(value.shape, right, jnp.int32) == 1, value, other)
            ref[at : at + count, :] = value
    blank = jnp.zeros((4, LANES), jnp.float32)
    column = jnp.concatenate(
        [den[0], den[1], reg[...].astype(jnp.float32), blank, mate_den[0], mate_den[1]]
        + [blank] * ((depth - 3 * TILE) // 4),
        0,
    )
    lane = lane_index(depth)
    mine = (lane >= COLUMN_LANE - COLUMN_K) & (lane < COLUMN_LANE + COLUMN_K)
    edges[0:depth, :] = jnp.where(mine, pltpu.roll(column, COLUMN_LANE, 1), packed[...])
    for n in range(3):
        at = plan.window_at + n * TILE
        edges[at : at + TILE, :] = pack(windows[16 * n : 16 * n + 16], WIN_K)
    for ref in (to_even, to_odd):
        at = sent.density
        ref[at : at + 3 * TILE, :] = column[: 3 * TILE]


def as_float(flag):
    return flag.astype(jnp.float32)


class Sides:
    def __init__(self, axis):
        index = lax.axis_index(axis)
        last = lax.axis_size(axis) - 1
        odd = lax.rem(index, 2)
        even = 1 - odd
        self.left = as_float(odd), as_float(even * (index > 0).astype(jnp.int32))
        self.right = as_float(even), as_float(odd * (index < last).astype(jnp.int32))

    @staticmethod
    def of(side, even, odd, at, count):
        return side[0] * even[at : at + count, :] + side[1] * odd[at : at + count, :]


class Rows:
    def __init__(self, depth, own, from_even, from_odd):
        self.sides = Sides("gx")
        self.sent = Sent(depth)
        self.depth = depth
        self.low, self.base = near_layers(depth)
        self.own = own
        self.even, self.odd = from_even, from_odd

    def of(self, row, at, count):
        side = self.sides.left if row < 0 else self.sides.right
        return self.sides.of(side, self.even, self.odd, at, count)

    def full(self, name, c, row):
        if 0 <= row < 4:
            return self.own[name][c, row]
        distance = -row if row < 0 else row - 3
        if (name, c, distance) not in self.sent.full:
            return jnp.zeros((self.depth, LANES), jnp.float32)
        return self.of(row, self.sent.full[name, c, distance], self.depth)

    def window(self, name, c, row):
        sent = self.sent
        if 0 <= row < 4:
            low = self.low - self.base if name in ("e", "h") else self.low
            return self.own[name][c, row, low : low + TILE, :]
        distance = -row if row < 0 else row - 3
        if (name, c, distance) in sent.full:
            return self.of(row, sent.full[name, c, distance] + self.low, TILE)
        if (name, c, distance) not in sent.pieces:
            return jnp.zeros((TILE, LANES), jnp.float32)
        at, count, from_left, from_right = sent.pieces[name, c, distance]
        at -= self.depth // 2 - self.low + (from_left if row < 0 else from_right)
        return self.of(row, at, TILE)


def combine_kernel(depth, odd, even, halo):
    plan = Edges(depth)
    sides = Sides("gy")
    for at, end, width in ((0, plan.window_at, FULL_K), (plan.window_at, plan.rows, WIN_K)):
        lane = lane_index(end - at)
        from_left = lax.rem(lane, 2 * width) >= width
        if at == 0:
            beside = (lane >= COLUMN_LANE - COLUMN_K) & (lane < COLUMN_LANE + COLUMN_K)
            from_left = jnp.where(beside, (lane < COLUMN_LANE).astype(jnp.int32), from_left.astype(jnp.int32)) == 1
        left = sides.of(sides.left, even, odd, at, end - at)
        right = sides.of(sides.right, even, odd, at, end - at)
        halo[at:end, :] = jnp.where(from_left, left, right)


def columns_kernel(depth, den, reg, from_odd, from_even, halo, halo_even, halo_odd, columns, far):
    sent = Sent(depth)
    sides = Sides("gx")
    odd = as_float(lax.rem(lax.axis_index("gx"), 2))
    count = 3 * TILE

    def beside(ref):
        return pltpu.roll(ref[0:count, :], LANES - COLUMN_LANE, 1)

    def within(ref):
        return ref[sent.density : sent.density + count, :]

    for lane, (own, even, away) in enumerate(
        ((None, within(from_even), within(from_odd)), (beside(halo), beside(halo_even), beside(halo_odd)))
    ):
        lanes = pl.ds(lane * LANES, LANES)
        below = sides.left[0] * even + sides.left[1] * away
        above = sides.right[0] * even + sides.right[1] * away
        zero_row = jnp.zeros((1, LANES), jnp.float32)
        mate = 2 * TILE
        for n in range(3):
            if own is None:
                here = den[n] if n < 2 else reg[...].astype(jnp.float32)
            else:
                here = own[4 * n : 4 * n + 4]
            to = 16 * n
            columns[to : to + 1, lanes] = zero_row
            columns[to + 15 : to + 16, lanes] = zero_row
            first = last = zero_row
            if n < 2:
                first = sides.left[1] * away[mate + 4 * n + 3 : mate + 4 * n + 4]
                last = sides.right[1] * away[mate + 4 * n : mate + 4 * n + 1]
                far[2 * n + lane : 2 * n + lane + 1, :] = (1.0 - odd) * below[4 * n + 3 : 4 * n + 4] + odd * above[4 * n : 4 * n + 1]
            columns[to + 1 : to + 2, lanes] = first
            columns[to + 2 : to + 6, lanes] = below[4 * n : 4 * n + 4]
            columns[to + 6 : to + 10, lanes] = here
            columns[to + 10 : to + 14, lanes] = above[4 * n : 4 * n + 4]
            columns[to + 14 : to + 15, lanes] = last
    far[4:8, :] = jnp.zeros((4, LANES), jnp.float32)


def up_z(block):
    depth = block.shape[0]
    moved = pltpu.roll(block, depth - 1, 0)
    if depth == TILE:
        return moved - block
    edge = lax.broadcasted_iota(jnp.int32, block.shape, 0) == depth - 1
    return jnp.where(edge, 0.0, moved) - block


def down_z(block):
    moved = pltpu.roll(block, 1, 0)
    if block.shape[0] == TILE:
        return block - moved
    edge = lax.broadcasted_iota(jnp.int32, block.shape, 0) == 0
    return block - jnp.where(edge, 0.0, moved)


def up_y(block):
    return pltpu.roll(block, block.shape[1] - 1, 1) - block


def down_y(block):
    return block - pltpu.roll(block, 1, 1)


def curl_up(here, after):
    x, y, z = here
    return (up_y(z) - up_z(y), up_z(x) - (after[2] - z), (after[1] - y) - up_y(x))


def curl_down(here, before):
    x, y, z = here
    return (down_y(z) - down_z(y), down_z(x) - (z - before[2]), (y - before[1]) - down_y(x))


def blur(block):
    table = kernel_table(RAD)
    lanes, count = block.shape[1], block.shape[0]
    sums = [block]
    for b in range(1, RAD + 1):
        sums.append(pltpu.roll(block, b, 1) + pltpu.roll(block, lanes - b, 1))
    total = None
    for a in range(RAD + 1):
        part = sum(float(table[RAD + a, RAD + b]) * sums[b] for b in range(RAD + 1))
        if a:
            part = pltpu.roll(part, a, 0) + pltpu.roll(part, count - a, 0)
        total = part if total is None else total + part
    return total


class Halos:
    def __init__(self, depth, x_sides, own, even, odd):
        self.depth = depth
        self.plan = Edges(depth)
        self.x_sides = x_sides
        self.own, self.even, self.odd = own, even, odd

    def of(self, row, at, count):
        if 0 <= row < 4:
            return self.own[at : at + count, :]
        side = self.x_sides.left if row < 0 else self.x_sides.right
        return self.x_sides.of(side, self.even, self.odd, at, count)

    def full(self, name, c, row):
        return unroll(self.of(row, 0, self.depth), self.plan.full_slot(name, c, row) * 2 * FULL_K)

    def window(self, name, c, row):
        at, slot = self.plan.window_slot(name, c, row)
        return unroll(self.of(row, self.plan.window_at + at, TILE), slot * 2 * WIN_K)


def unroll(block, shift):
    return pltpu.roll(block, LANES - shift, 1) if shift else block


class Coefficients:
    def __init__(self, region, densities):
        self.design = (region == 2.0).astype(jnp.float32)
        self.absorbing = (region == 1.0).astype(jnp.float32)
        self.source = (region == 3.0).astype(jnp.float32)
        self.inverse, self.slope = [], []
        for density in densities:
            inner = jnp.tanh(SHARP * (blur(density) - LEVEL))
            projected = (CREST + inner) / SCALE
            self.slope.append(SHARP * (1.0 - inner * inner) / SCALE)
            self.inverse.append(1.0 / (1.0 + CONTRAST * self.design * projected))
        damp = ABSORB * self.absorbing
        self.keep = (1.0 - damp) / (1.0 + damp)
        self.gain = COURANT / (1.0 + damp)


def inside_masks(x_sides, y_sides):
    lane = lane_index(TILE, 2 * LANES)
    inside = jnp.where(lane < LANES, 1.0, jnp.where(lane < LANES + LANES // 2, sum(y_sides.right), sum(y_sides.left)))
    return {"own": inside, "below": inside * sum(x_sides.left), "above": inside * sum(x_sides.right)}


def where_row(row):
    return "own" if 0 <= row < 4 else ("below" if row < 0 else "above")


def spread(block, row, count=TILE):
    at = row + DEN_BASE
    return jnp.broadcast_to(block[at : at + 1, :], (count, block.shape[1]))


def near_kernel(
    depth, columns, far, done_e, done_h, near,
    out_grad, out_e, out_h,
    grad, ratio_rows, sems,
):
    copies = [
        pltpu.make_async_copy(done_e, out_e, sems.at[0]),
        pltpu.make_async_copy(done_h, out_h, sems.at[1]),
        pltpu.make_async_copy(grad, out_grad, sems.at[2]),
    ]
    copies[0].start()
    copies[1].start()
    wide = 2 * LANES
    centre = depth // 2
    low = near_layers(depth)[0]

    def given(n, row):
        return [near[n, c, row + 3] for c in range(3)]

    odd = lax.rem(lax.axis_index("gx"), 2)
    far_at = jnp.where(odd == 1, DEN_BASE - 5, DEN_BASE + 8)
    at_far = lax.broadcasted_iota(jnp.int32, (16, wide), 0) == far_at
    densities = []
    for layer in range(2):
        row = jnp.concatenate([far[2 * layer : 2 * layer + 1, :], far[2 * layer + 1 : 2 * layer + 2, :]], 1)
        densities.append(jnp.where(at_far, jnp.broadcast_to(row, (16, wide)), columns[16 * layer : 16 * layer + 16, :]))
    known = Coefficients(columns[32:48, :], densities)
    inverse, slope, design, source = known.inverse, known.slope, known.design, known.source
    keep_col, gain_col = known.keep, known.gain
    masks = inside_masks(Sides("gx"), Sides("gy"))
    steps = {key: COURANT * value for key, value in masks.items()}

    sub = lax.broadcasted_iota(jnp.int32, (TILE, wide), 0) + low

    def layered(row):
        first, second = spread(inverse[0], row), spread(inverse[1], row)
        return jnp.where(sub == centre, first, jnp.where(sub == centre + 1, second, 1.0))

    keep_win = {row: spread(keep_col, row) for row in range(-3, 7)}
    layer_win = {row: layered(row) for row in range(-3, 7)}
    gain_win = {row: spread(gain_col, row) * layer_win[row] * masks[where_row(row)] for row in range(-3, 7)}
    source_plane = (sub == centre - 1).astype(jnp.float32)
    h1, e1, h2, drive1, drive2 = {}, {}, {}, {}, {}

    def minus_step(base, curl, row):
        step = steps[where_row(row)]
        return [b - step * c for b, c in zip(base, curl)]

    for row in range(-3, 7):
        h1[row], drive1[row] = given(0, row), given(1, row)
        e1[row] = [kept + gain_win[row] * d for kept, d in zip(given(2, row), drive1[row])]
    for row in range(-3, 6):
        h2[row] = minus_step(h1[row], curl_up(e1[row], e1[row + 1]), row)
    for row in range(-2, 6):
        drive2[row] = list(curl_down(h2[row], h2[row - 1]))
        drive2[row][2] = drive2[row][2] - math.sin(OMEGA * 2.0) * source_plane * spread(source, row)
    a2 = {row: given(3, row) for row in range(-3, 7)}
    ga_win = {row: [gain_win[row] * v for v in a2[row]] for row in range(-3, 7)}
    bh_win = {}
    for row in range(-3, 6):
        mask = masks[where_row(row)]
        curl = curl_up(ga_win[row], ga_win[row + 1])
        bh_win[row] = [v + mask * d for v, d in zip(given(4, row), curl)]
    ratio_rows[...] = jnp.zeros(ratio_rows.shape, jnp.float32)
    for row in range(-2, 6):
        a1 = minus_step(
            [keep_win[row] * v for v in a2[row]], curl_down(bh_win[row], bh_win[row - 1]), row
        )
        total = sum(a2[row][c] * drive2[row][c] + a1[c] * drive1[row][c] for c in range(3))
        for layer in range(2):
            at = centre + layer - low
            ratio_rows[layer, row + DEN_BASE : row + DEN_BASE + 1, :] = total[at : at + 1, :]
    for layer in range(2):
        sensitivity = -ratio_rows[layer] * gain_col * inverse[layer] * inverse[layer]
        smoothed = blur(CONTRAST * design * sensitivity * slope[layer])
        grad[layer] = smoothed[DEN_BASE : DEN_BASE + 4, :LANES]
    copies[2].start()
    for copy in copies:
        copy.wait()


def full_kernel(
    depth, e, h, ae, ah, from_even, from_odd, halo, halo_even, halo_odd, columns,
    out_e, out_h, near,
    ga, bh, be, gb,
):
    rows = Rows(depth, {"e": e, "h": h, "ae": ae, "ah": ah}, from_even, from_odd)
    halos = Halos(depth, rows.sides, halo, halo_even, halo_odd)
    wide = 2 * LANES
    centre = depth // 2

    def full(name, c, row):
        return jnp.concatenate([rows.full(name, c, row), halos.full(name, c, row)], 1)

    known = Coefficients(columns[32:48, :], [columns[16 * layer : 16 * layer + 16, :] for layer in range(2)])
    inverse, absorbing = known.inverse, known.absorbing
    masks = inside_masks(rows.sides, Sides("gy"))
    steps = {key: COURANT * value for key, value in masks.items()}

    def window(name, c, row):
        return jnp.concatenate([rows.window(name, c, row), halos.window(name, c, row)], 1)

    sub = lax.broadcasted_iota(jnp.int32, (TILE, wide), 0) + rows.low
    at_source = (sub == centre - 1).astype(jnp.float32) * math.sin(OMEGA)
    fields, magnetic = {}, {}
    for row in range(-4, 8):
        fields[row] = [window("e", c, row) for c in range(3)]
    for row in range(-4, 7):
        curl = curl_up(fields[row], fields[row + 1])
        magnetic[row] = [window("h", c, row) - steps[where_row(row)] * curl[c] for c in range(3)]
    for row in range(-3, 7):
        drive = list(curl_down(magnetic[row], magnetic[row - 1]))
        drive[2] = drive[2] - at_source * spread(known.source, row)
        keep = spread(known.keep, row)
        for c in range(3):
            near[0, c, row + 3] = magnetic[row][c]
            near[1, c, row + 3] = drive[c]
            near[2, c, row + 3] = keep * fields[row][c]
            near[3, c, row + 3] = window("ae", c, row)
            if row < 6:
                near[4, c, row + 3] = window("ah", c, row)

    z = lax.broadcasted_iota(jnp.int32, (depth, wide), 0)
    zf = z.astype(jnp.float32)
    margin = float(depth // 8)
    ramp = jnp.maximum(jnp.maximum((margin - zf) / margin, (zf - (depth - 1 - margin)) / margin), 0.0)
    open_damp = ABSORB * ramp * ramp
    full_damp = open_damp + ABSORB
    gain_open, gain_abs = COURANT / (1.0 + open_damp), COURANT / (1.0 + full_damp)
    keep_open, keep_abs = (1.0 - open_damp) / (1.0 + open_damp), (1.0 - full_damp) / (1.0 + full_damp)

    def coefficient(row):
        flag = spread(absorbing, row, depth) > 0.5
        layers = jnp.where(
            z == centre,
            spread(inverse[0], row, depth),
            jnp.where(z == centre + 1, spread(inverse[1], row, depth), 1.0),
        )
        return jnp.where(flag, keep_abs, keep_open), jnp.where(flag, gain_abs, gain_open) * layers

    def stretch(block):
        return jnp.broadcast_to(block[:1, :], (depth, wide))

    masks = {key: stretch(value) for key, value in masks.items()}
    steps = {key: stretch(value) for key, value in steps.items()}

    for row in range(-2, 6):
        keep, gain = coefficient(row)
        for c in range(3):
            value = full("ae", c, row)
            ga[c, row + 2] = gain * value
            if -1 <= row <= 4:
                be[c, row + 1] = keep * value
    for row in range(-2, 5):
        curl = curl_up([ga[c, row + 2] for c in range(3)], [ga[c, row + 3] for c in range(3)])
        for c in range(3):
            bh[c, row + 2] = full("ah", c, row) + masks[where_row(row)] * curl[c]
    for row in range(-1, 5):
        keep, gain = coefficient(row)
        curl = curl_down([bh[c, row + 2] for c in range(3)], [bh[c, row + 1] for c in range(3)])
        for c in range(3):
            value = be[c, row + 1] - steps[where_row(row)] * curl[c]
            be[c, row + 1] = keep * value
            gb[c, row + 1] = gain * value
    for row in range(-1, 4):
        curl = curl_up([gb[c, row + 1] for c in range(3)], [gb[c, row + 2] for c in range(3)])
        for c in range(3):
            value = bh[c, row + 2] + masks[where_row(row)] * curl[c]
            bh[c, row + 2] = value
            if row >= 0:
                out_h[c, row] = value[:, :LANES]
    for row in range(4):
        curl = curl_down([bh[c, row + 2] for c in range(3)], [bh[c, row + 1] for c in range(3)])
        for c in range(3):
            out_e[c, row] = be[c, row + 1][:, :LANES] - COURANT * curl[c][:, :LANES]


def per_device(density, e_field, h_field, adj_e, adj_h, region):
    depth = e_field.shape[2]
    sent, plan = Sent(depth), Edges(depth)
    f32 = jnp.float32
    params = pltpu.CompilerParams(vmem_limit_bytes=32 * 1024 * 1024)
    shape = jax.ShapeDtypeStruct
    near = e_field.shape[:2] + (2 * TILE, LANES)
    mate_den = pair_permute(density, x_even)
    own = pl.pallas_call(
        functools.partial(load_kernel, depth),
        out_shape=(
            pltpu.VMEM(density.shape, f32),
            pltpu.VMEM(near, f32),
            pltpu.VMEM(near, f32),
            pltpu.VMEM(adj_e.shape, f32),
            pltpu.VMEM(adj_h.shape, f32),
            pltpu.VMEM(region.shape, region.dtype),
            pltpu.VMEM((depth, LANES), f32),
        ),
        in_specs=[pl.BlockSpec(memory_space=pltpu.HBM)] * 6,
        scratch_shapes=[pltpu.SemaphoreType.DMA((6,))],
        compiler_params=pltpu.CompilerParams(vmem_limit_bytes=LOAD_VMEM),
        name="load",
    )(density, e_field, h_field, adj_e, adj_h, region)
    fields = own[1:5]
    edges, to_even, to_odd = pl.pallas_call(
        functools.partial(first_kernel, depth),
        out_shape=(
            shape((plan.rows, LANES), f32),
            shape((sent.rows, LANES), f32),
            shape((sent.rows, LANES), f32),
        ),
        compiler_params=params,
        name="first",
    )(*own, mate_den)
    edges_even = pair_permute(edges, y_even)
    edges_odd = pair_permute(edges, y_odd)
    from_odd = pair_permute(to_odd, x_ring)
    from_even = pair_permute(to_even, x_even)
    halo = pl.pallas_call(
        functools.partial(combine_kernel, depth),
        out_shape=shape((plan.rows, LANES), f32),
        compiler_params=params,
        name="combine",
    )(edges_odd, edges_even)
    halo_odd = pair_permute(halo, x_ring)
    halo_even = pair_permute(halo, x_even)
    wide = 2 * LANES
    columns, far = pl.pallas_call(
        functools.partial(columns_kernel, depth),
        out_shape=(shape((48, wide), f32), shape((TILE, LANES), f32)),
        compiler_params=params,
        name="columns",
    )(own[0], own[5], from_odd, from_even, halo, halo_even, halo_odd)
    far = pair_permute(far, x_even)
    done = pl.pallas_call(
        functools.partial(full_kernel, depth),
        out_shape=(
            pltpu.VMEM(e_field.shape, f32),
            pltpu.VMEM(e_field.shape, f32),
            pltpu.VMEM((5, 3, 10, TILE, wide), f32),
        ),
        scratch_shapes=[
            pltpu.VMEM((3, 8, depth, wide), f32),
            pltpu.VMEM((3, 7, depth, wide), f32),
            pltpu.VMEM((3, 6, depth, wide), f32),
            pltpu.VMEM((3, 6, depth, wide), f32),
        ],
        compiler_params=params,
        name="full",
    )(*fields, from_even, from_odd, halo, halo_even, halo_odd, columns)
    return pl.pallas_call(
        functools.partial(near_kernel, depth),
        out_shape=(shape(density.shape, f32), shape(e_field.shape, f32), shape(e_field.shape, f32)),
        out_specs=[pl.BlockSpec(memory_space=pltpu.HBM)] * 3,
        scratch_shapes=[
            pltpu.VMEM(density.shape, f32),
            pltpu.VMEM((2, 16, wide), f32),
            pltpu.SemaphoreType.DMA((3,)),
        ],
        compiler_params=params,
        name="near",
    )(columns, far, *done)


def solution(mesh):
    field = P(None, "gx", None, "gy")
    design = P(None, "gx", "gy")
    return jax.shard_map(
        per_device,
        mesh=mesh,
        in_specs=(design, field, field, field, field, P("gx", "gy")),
        out_specs=(design, field, field),
        check_vma=False,
    )
```

```python
import functools
import math

import jax
import jax.numpy as jnp
import numpy as np
from jax import lax
from jax.experimental import pallas as pl
from jax.experimental.pallas import tpu as pltpu
from jax.sharding import PartitionSpec as P

RAD = 2
COURANT = 0.5
SHARP = 4.0
LEVEL = 0.5
CONTRAST = 5.0
ABSORB = 0.3
OMEGA = 0.7
CREST = math.tanh(SHARP * LEVEL)
SCALE = CREST + math.tanh(SHARP * (1.0 - LEVEL))

LANES = 128
LOAD_VMEM = 56 * 1024 * 1024
TILE = 8
FULL_K = 2
WIN_K = 4
FIRST, LAST = -4, 8
DEN_BASE = 6


def kernel_table(radius):
    offsets = np.arange(-radius, radius + 1)
    distance = np.sqrt(offsets[:, None] ** 2 + offsets[None, :] ** 2)
    table = np.maximum(0.0, radius + 1.0 - distance)
    return table / table.sum()


def odd_swap(index):
    return ((index + 1) ^ 1) - 1


def pair_permute(block, partner):
    count_x, count_y = lax.axis_size("gx"), lax.axis_size("gy")
    route = []
    for i in range(count_x):
        for j in range(count_y):
            a, b = partner(i, j, count_x, count_y)
            route.append((i * count_y + j, a * count_y + b))
    return lax.ppermute(block, ("gx", "gy"), route)


def x_even(i, j, nx, ny):
    return i ^ 1, j


def x_odd(i, j, nx, ny):
    return (odd_swap(i), j) if 0 < i < nx - 1 else (i, j ^ 1)


def x_ring(i, j, nx, ny):
    if 0 < i < nx - 1:
        return odd_swap(i), j
    if i == 0:
        return (0, j - 1) if j > 0 else (nx - 1, j)
    return (i, j + 1) if j < ny - 1 else (0, j)


def y_even(i, j, nx, ny):
    return i, j ^ 1


def y_odd(i, j, nx, ny):
    return (i, odd_swap(j)) if 0 < j < ny - 1 else (i ^ 1, j)


PIECES = (
    ("e", 1, (0, 1, 2), 6, -2, -2),
    ("e", 2, (0, 1, 2), 6, -2, -2),
    ("e", 3, (0, 1, 2), 5, -1, -2),
    ("e", 4, (0, 1, 2), 4, 0, -2),
    ("h", 1, (0, 1, 2), 5, -2, -2),
    ("h", 2, (0, 1, 2), 5, -2, -2),
    ("h", 3, (0, 1, 2), 4, -1, -2),
    ("h", 4, (1, 2), 3, 0, 0),
    ("ae", 3, (0, 1, 2), 3, 0, -1),
    ("ah", 3, (1, 2), 2, 0, 0),
    ("ah", 2, (0,), 3, -1, -1),
)


class Sent:
    def __init__(self, depth):
        self.full = {}
        at = 0
        for name, far in (("ae", (0, 1, 2)), ("ah", (1, 2))):
            for distance in (1, 2):
                for c in (0, 1, 2) if distance == 1 else far:
                    self.full[name, c, distance] = at
                    at += depth
        self.pieces = {}
        for name, distance, components, count, left, right in PIECES:
            for c in components:
                self.pieces[name, c, distance] = at, count, left, right
                at += count
        at = -(-at // TILE) * TILE
        self.density = at
        self.region = at + TILE
        self.mate = at + 2 * TILE
        self.rows = at + 3 * TILE


FIELDS = ("ae", "ah", "e", "h")


COLUMN_K = 8
COLUMN_LANE = 104


class Edges:
    def __init__(self, depth):
        self.window_at = depth
        self.rows = depth + 3 * TILE
        self.density, self.region, self.mate = 0, TILE, 2 * TILE

    def full_slot(self, name, c, row):
        return row % 4 * 6 + FIELDS.index(name) * 3 + c

    def window_slot(self, name, c, row):
        place = (FIELDS.index(name) * 3 + c) * 4 + row % 4
        return place // 16 * TILE, place % 16


def lane_index(rows, lanes=LANES):
    return lax.broadcasted_iota(jnp.int32, (rows, lanes), 1)


def pack(planes, width):
    slots = LANES // (2 * width)
    owner = lax.rem((lane_index(planes[0].shape[0]) + width) // (2 * width), slots)
    total = None
    for slot, plane in enumerate(planes):
        moved = pltpu.roll(plane, slot * 2 * width, 1) if slot else plane
        total = moved if total is None else jnp.where(owner == slot, moved, total)
    return total


def near_layers(depth):
    low = depth // 2 - 4
    return low, low // TILE * TILE


def load_kernel(depth, den, e, h, ae, ah, reg, own_den, own_e, own_h, own_ae, own_ah, own_reg, packed, sems):
    near = pl.ds(near_layers(depth)[1], 2 * TILE)
    pairs = [(ae.at[c], own_ae.at[c]) for c in range(3)]
    pairs += [(ah.at[c], own_ah.at[c]) for c in range(3)]
    pairs += [(e.at[:, :, near, :], own_e), (h.at[:, :, near, :], own_h), (den, own_den), (reg, own_reg)]
    copies = [pltpu.make_async_copy(source, target, sems.at[n]) for n, (source, target) in enumerate(pairs)]
    for copy in copies:
        copy.start()
    for copy in copies[:6]:
        copy.wait()
    own = (own_ae, own_ah)
    packed[...] = pack([field[c, row] for row in range(4) for field in own for c in range(3)], FULL_K)
    for copy in copies[6:]:
        copy.wait()


def near_windows(depth, e, h, ae, ah):
    low, base = near_layers(depth)
    windows = []
    for field, start in ((ae, low), (ah, low), (e, low - base), (h, low - base)):
        for c in range(3):
            for row in range(4):
                windows.append(field[c, row, start : start + TILE, :])
    return windows


def first_kernel(depth, den, e, h, ae, ah, reg, packed, mate_den, edges, to_even, to_odd):
    plan, sent = Edges(depth), Sent(depth)
    low = near_layers(depth)[0]
    odd = lax.rem(lax.axis_index("gx"), 2)
    own = {"ae": ae, "ah": ah}
    windows = near_windows(depth, e, h, ae, ah)
    centre = depth // 2
    base = near_layers(depth)[1]
    fields = {"ae": (ae, centre), "ah": (ah, centre), "e": (e, centre - base), "h": (h, centre - base)}
    for ref, right in ((to_even, 1 - odd), (to_odd, odd)):
        row_of = lambda distance: right * (ae.shape[1] + 1 - 2 * distance) + distance - 1
        for (name, c, distance), at in sent.full.items():
            ref[at : at + depth, :] = own[name][c, row_of(distance)]
        for (name, c, distance), (at, count, from_left, from_right) in sent.pieces.items():
            field, middle = fields[name]
            row = row_of(distance)
            value = field[c, row, middle + from_left : middle + from_left + count, :]
            if from_left != from_right:
                other = field[c, row, middle + from_right : middle + from_right + count, :]
                value = jnp.where(jnp.full(value.shape, right, jnp.int32) == 1, value, other)
            ref[at : at + count, :] = value
    blank = jnp.zeros((4, LANES), jnp.float32)
    column = jnp.concatenate(
        [den[0], den[1], reg[...].astype(jnp.float32), blank, mate_den[0], mate_den[1]]
        + [blank] * ((depth - 3 * TILE) // 4),
        0,
    )
    lane = lane_index(depth)
    mine = (lane >= COLUMN_LANE - COLUMN_K) & (lane < COLUMN_LANE + COLUMN_K)
    edges[0:depth, :] = jnp.where(mine, pltpu.roll(column, COLUMN_LANE, 1), packed[...])
    for n in range(3):
        at = plan.window_at + n * TILE
        edges[at : at + TILE, :] = pack(windows[16 * n : 16 * n + 16], WIN_K)
    for ref in (to_even, to_odd):
        at = sent.density
        ref[at : at + 3 * TILE, :] = column[: 3 * TILE]


def as_float(flag):
    return flag.astype(jnp.float32)


class Sides:
    def __init__(self, axis):
        index = lax.axis_index(axis)
        last = lax.axis_size(axis) - 1
        odd = lax.rem(index, 2)
        even = 1 - odd
        self.left = as_float(odd), as_float(even * (index > 0).astype(jnp.int32))
        self.right = as_float(even), as_float(odd * (index < last).astype(jnp.int32))

    @staticmethod
    def of(side, even, odd, at, count):
        return side[0] * even[at : at + count, :] + side[1] * odd[at : at + count, :]


class Rows:
    def __init__(self, depth, own, from_even, from_odd):
        self.sides = Sides("gx")
        self.sent = Sent(depth)
        self.depth = depth
        self.low, self.base = near_layers(depth)
        self.own = own
        self.even, self.odd = from_even, from_odd

    def of(self, row, at, count):
        side = self.sides.left if row < 0 else self.sides.right
        return self.sides.of(side, self.even, self.odd, at, count)

    def full(self, name, c, row):
        if 0 <= row < 4:
            return self.own[name][c, row]
        distance = -row if row < 0 else row - 3
        if (name, c, distance) not in self.sent.full:
            return jnp.zeros((self.depth, LANES), jnp.float32)
        return self.of(row, self.sent.full[name, c, distance], self.depth)

    def window(self, name, c, row):
        sent = self.sent
        if 0 <= row < 4:
            low = self.low - self.base if name in ("e", "h") else self.low
            return self.own[name][c, row, low : low + TILE, :]
        distance = -row if row < 0 else row - 3
        if (name, c, distance) in sent.full:
            return self.of(row, sent.full[name, c, distance] + self.low, TILE)
        if (name, c, distance) not in sent.pieces:
            return jnp.zeros((TILE, LANES), jnp.float32)
        at, count, from_left, from_right = sent.pieces[name, c, distance]
        at -= self.depth // 2 - self.low + (from_left if row < 0 else from_right)
        return self.of(row, at, TILE)


def combine_kernel(depth, odd, even, halo):
    plan = Edges(depth)
    sides = Sides("gy")
    for at, end, width in ((0, plan.window_at, FULL_K), (plan.window_at, plan.rows, WIN_K)):
        lane = lane_index(end - at)
        from_left = lax.rem(lane, 2 * width) >= width
        if at == 0:
            beside = (lane >= COLUMN_LANE - COLUMN_K) & (lane < COLUMN_LANE + COLUMN_K)
            from_left = jnp.where(beside, (lane < COLUMN_LANE).astype(jnp.int32), from_left.astype(jnp.int32)) == 1
        left = sides.of(sides.left, even, odd, at, end - at)
        right = sides.of(sides.right, even, odd, at, end - at)
        halo[at:end, :] = jnp.where(from_left, left, right)


def columns_kernel(depth, den, reg, from_odd, from_even, halo, halo_even, halo_odd, columns, far):
    sent = Sent(depth)
    sides = Sides("gx")
    odd = as_float(lax.rem(lax.axis_index("gx"), 2))
    count = 3 * TILE

    def beside(ref):
        return pltpu.roll(ref[0:count, :], LANES - COLUMN_LANE, 1)

    def within(ref):
        return ref[sent.density : sent.density + count, :]

    for lane, (own, even, away) in enumerate(
        ((None, within(from_even), within(from_odd)), (beside(halo), beside(halo_even), beside(halo_odd)))
    ):
        lanes = pl.ds(lane * LANES, LANES)
        below = sides.left[0] * even + sides.left[1] * away
        above = sides.right[0] * even + sides.right[1] * away
        zero_row = jnp.zeros((1, LANES), jnp.float32)
        mate = 2 * TILE
        for n in range(3):
            if own is None:
                here = den[n] if n < 2 else reg[...].astype(jnp.float32)
            else:
                here = own[4 * n : 4 * n + 4]
            to = 16 * n
            columns[to : to + 1, lanes] = zero_row
            columns[to + 15 : to + 16, lanes] = zero_row
            first = last = zero_row
            if n < 2:
                first = sides.left[1] * away[mate + 4 * n + 3 : mate + 4 * n + 4]
                last = sides.right[1] * away[mate + 4 * n : mate + 4 * n + 1]
                far[2 * n + lane : 2 * n + lane + 1, :] = (1.0 - odd) * below[4 * n + 3 : 4 * n + 4] + odd * above[4 * n : 4 * n + 1]
            columns[to + 1 : to + 2, lanes] = first
            columns[to + 2 : to + 6, lanes] = below[4 * n : 4 * n + 4]
            columns[to + 6 : to + 10, lanes] = here
            columns[to + 10 : to + 14, lanes] = above[4 * n : 4 * n + 4]
            columns[to + 14 : to + 15, lanes] = last
    far[4:8, :] = jnp.zeros((4, LANES), jnp.float32)


def up_z(block):
    depth = block.shape[0]
    moved = pltpu.roll(block, depth - 1, 0)
    if depth == TILE:
        return moved - block
    edge = lax.broadcasted_iota(jnp.int32, block.shape, 0) == depth - 1
    return jnp.where(edge, 0.0, moved) - block


def down_z(block):
    moved = pltpu.roll(block, 1, 0)
    if block.shape[0] == TILE:
        return block - moved
    edge = lax.broadcasted_iota(jnp.int32, block.shape, 0) == 0
    return block - jnp.where(edge, 0.0, moved)


def up_y(block):
    return pltpu.roll(block, block.shape[1] - 1, 1) - block


def down_y(block):
    return block - pltpu.roll(block, 1, 1)


def curl_up(here, after):
    x, y, z = here
    return (up_y(z) - up_z(y), up_z(x) - (after[2] - z), (after[1] - y) - up_y(x))


def curl_down(here, before):
    x, y, z = here
    return (down_y(z) - down_z(y), down_z(x) - (z - before[2]), (y - before[1]) - down_y(x))


def blur(block):
    table = kernel_table(RAD)
    lanes, count = block.shape[1], block.shape[0]
    sums = [block]
    for b in range(1, RAD + 1):
        sums.append(pltpu.roll(block, b, 1) + pltpu.roll(block, lanes - b, 1))
    total = None
    for a in range(RAD + 1):
        part = sum(float(table[RAD + a, RAD + b]) * sums[b] for b in range(RAD + 1))
        if a:
            part = pltpu.roll(part, a, 0) + pltpu.roll(part, count - a, 0)
        total = part if total is None else total + part
    return total


class Halos:
    def __init__(self, depth, x_sides, own, even, odd):
        self.depth = depth
        self.plan = Edges(depth)
        self.x_sides = x_sides
        self.own, self.even, self.odd = own, even, odd

    def of(self, row, at, count):
        if 0 <= row < 4:
            return self.own[at : at + count, :]
        side = self.x_sides.left if row < 0 else self.x_sides.right
        return self.x_sides.of(side, self.even, self.odd, at, count)

    def full(self, name, c, row):
        return unroll(self.of(row, 0, self.depth), self.plan.full_slot(name, c, row) * 2 * FULL_K)

    def window(self, name, c, row):
        at, slot = self.plan.window_slot(name, c, row)
        return unroll(self.of(row, self.plan.window_at + at, TILE), slot * 2 * WIN_K)


def unroll(block, shift):
    return pltpu.roll(block, LANES - shift, 1) if shift else block


class Coefficients:
    def __init__(self, region, densities):
        self.design = (region == 2.0).astype(jnp.float32)
        self.absorbing = (region == 1.0).astype(jnp.float32)
        self.source = (region == 3.0).astype(jnp.float32)
        self.inverse, self.slope = [], []
        for density in densities:
            inner = jnp.tanh(SHARP * (blur(density) - LEVEL))
            projected = (CREST + inner) / SCALE
            self.slope.append(SHARP * (1.0 - inner * inner) / SCALE)
            self.inverse.append(1.0 / (1.0 + CONTRAST * self.design * projected))
        damp = ABSORB * self.absorbing
        self.keep = (1.0 - damp) / (1.0 + damp)
        self.gain = COURANT / (1.0 + damp)


def inside_masks(x_sides, y_sides):
    lane = lane_index(TILE, 2 * LANES)
    inside = jnp.where(lane < LANES, 1.0, jnp.where(lane < LANES + LANES // 2, sum(y_sides.right), sum(y_sides.left)))
    return {"own": inside, "below": inside * sum(x_sides.left), "above": inside * sum(x_sides.right)}


def where_row(row):
    return "own" if 0 <= row < 4 else ("below" if row < 0 else "above")


def spread(block, row, count=TILE):
    at = row + DEN_BASE
    return jnp.broadcast_to(block[at : at + 1, :], (count, block.shape[1]))


def near_kernel(
    depth, columns, far, done_e, done_h, near,
    out_grad, out_e, out_h,
    grad, ratio_rows, sems,
):
    copies = [
        pltpu.make_async_copy(done_e, out_e, sems.at[0]),
        pltpu.make_async_copy(done_h, out_h, sems.at[1]),
        pltpu.make_async_copy(grad, out_grad, sems.at[2]),
    ]
    copies[0].start()
    copies[1].start()
    wide = 2 * LANES
    centre = depth // 2
    low = near_layers(depth)[0]

    def given(n, row):
        return [near[n, c, row + 3] for c in range(3)]

    odd = lax.rem(lax.axis_index("gx"), 2)
    far_at = jnp.where(odd == 1, DEN_BASE - 5, DEN_BASE + 8)
    at_far = lax.broadcasted_iota(jnp.int32, (16, wide), 0) == far_at
    densities = []
    for layer in range(2):
        row = jnp.concatenate([far[2 * layer : 2 * layer + 1, :], far[2 * layer + 1 : 2 * layer + 2, :]], 1)
        densities.append(jnp.where(at_far, jnp.broadcast_to(row, (16, wide)), columns[16 * layer : 16 * layer + 16, :]))
    known = Coefficients(columns[32:48, :], densities)
    inverse, slope, design, source = known.inverse, known.slope, known.design, known.source
    keep_col, gain_col = known.keep, known.gain
    masks = inside_masks(Sides("gx"), Sides("gy"))
    steps = {key: COURANT * value for key, value in masks.items()}

    sub = lax.broadcasted_iota(jnp.int32, (TILE, wide), 0) + low

    def layered(row):
        first, second = spread(inverse[0], row), spread(inverse[1], row)
        return jnp.where(sub == centre, first, jnp.where(sub == centre + 1, second, 1.0))

    keep_win = {row: spread(keep_col, row) for row in range(-3, 7)}
    layer_win = {row: layered(row) for row in range(-3, 7)}
    gain_win = {row: spread(gain_col, row) * layer_win[row] * masks[where_row(row)] for row in range(-3, 7)}
    source_plane = (sub == centre - 1).astype(jnp.float32)
    h1, e1, h2, drive1, drive2 = {}, {}, {}, {}, {}

    def minus_step(base, curl, row):
        step = steps[where_row(row)]
        return [b - step * c for b, c in zip(base, curl)]

    for row in range(-3, 7):
        h1[row], drive1[row] = given(0, row), given(1, row)
        e1[row] = [kept + gain_win[row] * d for kept, d in zip(given(2, row), drive1[row])]
    for row in range(-3, 6):
        h2[row] = minus_step(h1[row], curl_up(e1[row], e1[row + 1]), row)
    for row in range(-2, 6):
        drive2[row] = list(curl_down(h2[row], h2[row - 1]))
        drive2[row][2] = drive2[row][2] - math.sin(OMEGA * 2.0) * source_plane * spread(source, row)
    a2 = {row: given(3, row) for row in range(-3, 7)}
    ga_win = {row: [gain_win[row] * v for v in a2[row]] for row in range(-3, 7)}
    bh_win = {}
    for row in range(-3, 6):
        mask = masks[where_row(row)]
        curl = curl_up(ga_win[row], ga_win[row + 1])
        bh_win[row] = [v + mask * d for v, d in zip(given(4, row), curl)]
    ratio_rows[...] = jnp.zeros(ratio_rows.shape, jnp.float32)
    for row in range(-2, 6):
        a1 = minus_step(
            [keep_win[row] * v for v in a2[row]], curl_down(bh_win[row], bh_win[row - 1]), row
        )
        total = sum(a2[row][c] * drive2[row][c] + a1[c] * drive1[row][c] for c in range(3))
        for layer in range(2):
            at = centre + layer - low
            ratio_rows[layer, row + DEN_BASE : row + DEN_BASE + 1, :] = total[at : at + 1, :]
    for layer in range(2):
        sensitivity = -ratio_rows[layer] * gain_col * inverse[layer] * inverse[layer]
        smoothed = blur(CONTRAST * design * sensitivity * slope[layer])
        grad[layer] = smoothed[DEN_BASE : DEN_BASE + 4, :LANES]
    copies[2].start()
    for copy in copies:
        copy.wait()


def full_kernel(
    depth, e, h, ae, ah, from_even, from_odd, halo, halo_even, halo_odd, columns,
    out_e, out_h, near,
    ga, bh, be, gb,
):
    rows = Rows(depth, {"e": e, "h": h, "ae": ae, "ah": ah}, from_even, from_odd)
    halos = Halos(depth, rows.sides, halo, halo_even, halo_odd)
    wide = 2 * LANES
    centre = depth // 2

    def full(name, c, row):
        return jnp.concatenate([rows.full(name, c, row), halos.full(name, c, row)], 1)

    known = Coefficients(columns[32:48, :], [columns[16 * layer : 16 * layer + 16, :] for layer in range(2)])
    inverse, absorbing = known.inverse, known.absorbing
    masks = inside_masks(rows.sides, Sides("gy"))
    steps = {key: COURANT * value for key, value in masks.items()}

    def window(name, c, row):
        return jnp.concatenate([rows.window(name, c, row), halos.window(name, c, row)], 1)

    sub = lax.broadcasted_iota(jnp.int32, (TILE, wide), 0) + rows.low
    at_source = (sub == centre - 1).astype(jnp.float32) * math.sin(OMEGA)
    fields, magnetic = {}, {}
    for row in range(-4, 8):
        fields[row] = [window("e", c, row) for c in range(3)]
    for row in range(-4, 7):
        curl = curl_up(fields[row], fields[row + 1])
        magnetic[row] = [window("h", c, row) - steps[where_row(row)] * curl[c] for c in range(3)]
    for row in range(-3, 7):
        drive = list(curl_down(magnetic[row], magnetic[row - 1]))
        drive[2] = drive[2] - at_source * spread(known.source, row)
        keep = spread(known.keep, row)
        for c in range(3):
            near[0, c, row + 3] = magnetic[row][c]
            near[1, c, row + 3] = drive[c]
            near[2, c, row + 3] = keep * fields[row][c]
            near[3, c, row + 3] = window("ae", c, row)
            if row < 6:
                near[4, c, row + 3] = window("ah", c, row)

    z = lax.broadcasted_iota(jnp.int32, (depth, wide), 0)
    zf = z.astype(jnp.float32)
    margin = float(depth // 8)
    ramp = jnp.maximum(jnp.maximum((margin - zf) / margin, (zf - (depth - 1 - margin)) / margin), 0.0)
    open_damp = ABSORB * ramp * ramp
    full_damp = open_damp + ABSORB
    gain_open, gain_abs = COURANT / (1.0 + open_damp), COURANT / (1.0 + full_damp)
    keep_open, keep_abs = (1.0 - open_damp) / (1.0 + open_damp), (1.0 - full_damp) / (1.0 + full_damp)

    def coefficient(row):
        flag = spread(absorbing, row, depth) > 0.5
        layers = jnp.where(
            z == centre,
            spread(inverse[0], row, depth),
            jnp.where(z == centre + 1, spread(inverse[1], row, depth), 1.0),
        )
        return jnp.where(flag, keep_abs, keep_open), jnp.where(flag, gain_abs, gain_open) * layers

    def stretch(block):
        return jnp.broadcast_to(block[:1, :], (depth, wide))

    masks = {key: stretch(value) for key, value in masks.items()}
    steps = {key: stretch(value) for key, value in steps.items()}

    for row in range(-2, 6):
        keep, gain = coefficient(row)
        for c in range(3):
            value = full("ae", c, row)
            ga[c, row + 2] = gain * value
            if -1 <= row <= 4:
                be[c, row + 1] = keep * value
    for row in range(-2, 5):
        curl = curl_up([ga[c, row + 2] for c in range(3)], [ga[c, row + 3] for c in range(3)])
        for c in range(3):
            bh[c, row + 2] = full("ah", c, row) + masks[where_row(row)] * curl[c]
    for row in range(-1, 5):
        keep, gain = coefficient(row)
        curl = curl_down([bh[c, row + 2] for c in range(3)], [bh[c, row + 1] for c in range(3)])
        for c in range(3):
            value = be[c, row + 1] - steps[where_row(row)] * curl[c]
            be[c, row + 1] = keep * value
            gb[c, row + 1] = gain * value
    for row in range(-1, 4):
        curl = curl_up([gb[c, row + 1] for c in range(3)], [gb[c, row + 2] for c in range(3)])
        for c in range(3):
            value = bh[c, row + 2] + masks[where_row(row)] * curl[c]
            bh[c, row + 2] = value
            if row >= 0:
                out_h[c, row] = value[:, :LANES]
    for row in range(4):
        curl = curl_down([bh[c, row + 2] for c in range(3)], [bh[c, row + 1] for c in range(3)])
        for c in range(3):
            out_e[c, row] = be[c, row + 1][:, :LANES] - COURANT * curl[c][:, :LANES]


def per_device(density, e_field, h_field, adj_e, adj_h, region):
    depth = e_field.shape[2]
    sent, plan = Sent(depth), Edges(depth)
    f32 = jnp.float32
    params = pltpu.CompilerParams(vmem_limit_bytes=32 * 1024 * 1024)
    shape = jax.ShapeDtypeStruct
    near = e_field.shape[:2] + (2 * TILE, LANES)
    mate_den = pair_permute(density, x_even)
    own = pl.pallas_call(
        functools.partial(load_kernel, depth),
        out_shape=(
            pltpu.VMEM(density.shape, f32),
            pltpu.VMEM(near, f32),
            pltpu.VMEM(near, f32),
            pltpu.VMEM(adj_e.shape, f32),
            pltpu.VMEM(adj_h.shape, f32),
            pltpu.VMEM(region.shape, region.dtype),
            pltpu.VMEM((depth, LANES), f32),
        ),
        in_specs=[pl.BlockSpec(memory_space=pltpu.HBM)] * 6,
        scratch_shapes=[pltpu.SemaphoreType.DMA((10,))],
        compiler_params=pltpu.CompilerParams(vmem_limit_bytes=LOAD_VMEM),
        name="load",
    )(density, e_field, h_field, adj_e, adj_h, region)
    fields = own[1:5]
    edges, to_even, to_odd = pl.pallas_call(
        functools.partial(first_kernel, depth),
        out_shape=(
            shape((plan.rows, LANES), f32),
            shape((sent.rows, LANES), f32),
            shape((sent.rows, LANES), f32),
        ),
        compiler_params=params,
        name="first",
    )(*own, mate_den)
    edges_even = pair_permute(edges, y_even)
    edges_odd = pair_permute(edges, y_odd)
    from_odd = pair_permute(to_odd, x_ring)
    from_even = pair_permute(to_even, x_even)
    halo = pl.pallas_call(
        functools.partial(combine_kernel, depth),
        out_shape=shape((plan.rows, LANES), f32),
        compiler_params=params,
        name="combine",
    )(edges_odd, edges_even)
    halo_odd = pair_permute(halo, x_odd)
    halo_even = pair_permute(halo, x_even)
    wide = 2 * LANES
    columns, far = pl.pallas_call(
        functools.partial(columns_kernel, depth),
        out_shape=(shape((48, wide), f32), shape((TILE, LANES), f32)),
        compiler_params=params,
        name="columns",
    )(own[0], own[5], from_odd, from_even, halo, halo_even, halo_odd)
    far = pair_permute(far, x_even)
    done = pl.pallas_call(
        functools.partial(full_kernel, depth),
        out_shape=(
            pltpu.VMEM(e_field.shape, f32),
            pltpu.VMEM(e_field.shape, f32),
            pltpu.VMEM((5, 3, 10, TILE, wide), f32),
        ),
        scratch_shapes=[
            pltpu.VMEM((3, 8, depth, wide), f32),
            pltpu.VMEM((3, 7, depth, wide), f32),
            pltpu.VMEM((3, 6, depth, wide), f32),
            pltpu.VMEM((3, 6, depth, wide), f32),
        ],
        compiler_params=params,
        name="full",
    )(*fields, from_even, from_odd, halo, halo_even, halo_odd, columns)
    return pl.pallas_call(
        functools.partial(near_kernel, depth),
        out_shape=(shape(density.shape, f32), shape(e_field.shape, f32), shape(e_field.shape, f32)),
        out_specs=[pl.BlockSpec(memory_space=pltpu.HBM)] * 3,
        scratch_shapes=[
            pltpu.VMEM(density.shape, f32),
            pltpu.VMEM((2, 16, wide), f32),
            pltpu.SemaphoreType.DMA((3,)),
        ],
        compiler_params=params,
        name="near",
    )(columns, far, *done)


def solution(mesh):
    field = P(None, "gx", None, "gy")
    design = P(None, "gx", "gy")
    return jax.shard_map(
        per_device,
        mesh=mesh,
        in_specs=(design, field, field, field, field, P("gx", "gy")),
        out_specs=(design, field, field),
        check_vma=False,
    )
```

```python
import functools
import math

import jax
import jax.numpy as jnp
import numpy as np
from jax import lax
from jax.experimental import pallas as pl
from jax.experimental.pallas import tpu as pltpu
from jax.sharding import PartitionSpec as P

RAD = 2
COURANT = 0.5
SHARP = 4.0
LEVEL = 0.5
CONTRAST = 5.0
ABSORB = 0.3
OMEGA = 0.7
CREST = math.tanh(SHARP * LEVEL)
SCALE = CREST + math.tanh(SHARP * (1.0 - LEVEL))

LANES = 128
LOAD_VMEM = 56 * 1024 * 1024
TILE = 8
FULL_K = 2
WIN_K = 4
FIRST, LAST = -4, 8
DEN_BASE = 6


def kernel_table(radius):
    offsets = np.arange(-radius, radius + 1)
    distance = np.sqrt(offsets[:, None] ** 2 + offsets[None, :] ** 2)
    table = np.maximum(0.0, radius + 1.0 - distance)
    return table / table.sum()


def odd_swap(index):
    return ((index + 1) ^ 1) - 1


def pair_permute(block, partner):
    count_x, count_y = lax.axis_size("gx"), lax.axis_size("gy")
    route = []
    for i in range(count_x):
        for j in range(count_y):
            a, b = partner(i, j, count_x, count_y)
            route.append((i * count_y + j, a * count_y + b))
    return lax.ppermute(block, ("gx", "gy"), route)


def x_even(i, j, nx, ny):
    return i ^ 1, j


def x_odd(i, j, nx, ny):
    return (odd_swap(i), j) if 0 < i < nx - 1 else (i, j ^ 1)


def x_ring(i, j, nx, ny):
    if 0 < i < nx - 1:
        return odd_swap(i), j
    if i == 0:
        return (0, j - 1) if j > 0 else (nx - 1, j)
    return (i, j + 1) if j < ny - 1 else (0, j)


def y_even(i, j, nx, ny):
    return i, j ^ 1


def y_odd(i, j, nx, ny):
    return (i, odd_swap(j)) if 0 < j < ny - 1 else (i ^ 1, j)


PIECES = (
    ("e", 1, (0, 1, 2), 6, -2, -2),
    ("e", 2, (0, 1, 2), 6, -2, -2),
    ("e", 3, (0, 1, 2), 5, -1, -2),
    ("e", 4, (0, 1, 2), 4, 0, -2),
    ("h", 1, (0, 1, 2), 5, -2, -2),
    ("h", 2, (0, 1, 2), 5, -2, -2),
    ("h", 3, (0, 1, 2), 4, -1, -2),
    ("h", 4, (1, 2), 3, 0, 0),
    ("ae", 3, (0, 1, 2), 3, 0, -1),
    ("ah", 3, (1, 2), 2, 0, 0),
    ("ah", 2, (0,), 3, -1, -1),
)


class Sent:
    def __init__(self, depth):
        self.full = {}
        at = 0
        for name, far in (("ae", (0, 1, 2)), ("ah", (1, 2))):
            for distance in (1, 2):
                for c in (0, 1, 2) if distance == 1 else far:
                    self.full[name, c, distance] = at
                    at += depth
        self.pieces = {}
        for name, distance, components, count, left, right in PIECES:
            for c in components:
                self.pieces[name, c, distance] = at, count, left, right
                at += count
        at = -(-at // TILE) * TILE
        self.density = at
        self.region = at + TILE
        self.mate = at + 2 * TILE
        self.rows = at + 3 * TILE


FIELDS = ("ae", "ah", "e", "h")


COLUMN_K = 8
COLUMN_LANE = 104


class Edges:
    def __init__(self, depth):
        self.window_at = depth
        self.rows = depth + 3 * TILE
        self.density, self.region, self.mate = 0, TILE, 2 * TILE

    def full_slot(self, name, c, row):
        return row % 4 * 6 + FIELDS.index(name) * 3 + c

    def window_slot(self, name, c, row):
        place = (FIELDS.index(name) * 3 + c) * 4 + row % 4
        return place // 16 * TILE, place % 16


def lane_index(rows, lanes=LANES):
    return lax.broadcasted_iota(jnp.int32, (rows, lanes), 1)


def pack(planes, width):
    slots = LANES // (2 * width)
    owner = lax.rem((lane_index(planes[0].shape[0]) + width) // (2 * width), slots)
    total = None
    for slot, plane in enumerate(planes):
        moved = pltpu.roll(plane, slot * 2 * width, 1) if slot else plane
        total = moved if total is None else jnp.where(owner == slot, moved, total)
    return total


def near_layers(depth):
    low = depth // 2 - 4
    return low, low // TILE * TILE


def load_kernel(depth, den, e, h, ae, ah, reg, own_den, own_e, own_h, own_ae, own_ah, own_reg, packed, sems):
    near = pl.ds(near_layers(depth)[1], 2 * TILE)
    pairs = (
        (ae, own_ae),
        (ah, own_ah),
        (e.at[:, :, near, :], own_e),
        (h.at[:, :, near, :], own_h),
        (den, own_den),
        (reg, own_reg),
    )
    copies = [pltpu.make_async_copy(source, target, sems.at[n]) for n, (source, target) in enumerate(pairs)]
    for copy in copies:
        copy.start()
    copies[0].wait()
    copies[1].wait()
    own = (own_ae, own_ah)
    packed[...] = pack([field[c, row] for row in range(4) for field in own for c in range(3)], FULL_K)
    for copy in copies[2:]:
        copy.wait()


def near_windows(depth, e, h, ae, ah):
    low, base = near_layers(depth)
    windows = []
    for field, start in ((ae, low), (ah, low), (e, low - base), (h, low - base)):
        for c in range(3):
            for row in range(4):
                windows.append(field[c, row, start : start + TILE, :])
    return windows


def first_kernel(depth, den, e, h, ae, ah, reg, packed, mate_den, edges, to_even, to_odd):
    plan, sent = Edges(depth), Sent(depth)
    low = near_layers(depth)[0]
    odd = lax.rem(lax.axis_index("gx"), 2)
    own = {"ae": ae, "ah": ah}
    windows = near_windows(depth, e, h, ae, ah)
    centre = depth // 2
    base = near_layers(depth)[1]
    fields = {"ae": (ae, centre), "ah": (ah, centre), "e": (e, centre - base), "h": (h, centre - base)}
    for ref, right in ((to_even, 1 - odd), (to_odd, odd)):
        row_of = lambda distance: right * (ae.shape[1] + 1 - 2 * distance) + distance - 1
        for (name, c, distance), at in sent.full.items():
            ref[at : at + depth, :] = own[name][c, row_of(distance)]
        for (name, c, distance), (at, count, from_left, from_right) in sent.pieces.items():
            field, middle = fields[name]
            row = row_of(distance)
            value = field[c, row, middle + from_left : middle + from_left + count, :]
            if from_left != from_right:
                other = field[c, row, middle + from_right : middle + from_right + count, :]
                value = jnp.where(jnp.full(value.shape, right, jnp.int32) == 1, value, other)
            ref[at : at + count, :] = value
    blank = jnp.zeros((4, LANES), jnp.float32)
    column = jnp.concatenate(
        [den[0], den[1], reg[...].astype(jnp.float32), blank, mate_den[0], mate_den[1]]
        + [blank] * ((depth - 3 * TILE) // 4),
        0,
    )
    lane = lane_index(depth)
    mine = (lane >= COLUMN_LANE - COLUMN_K) & (lane < COLUMN_LANE + COLUMN_K)
    edges[0:depth, :] = jnp.where(mine, pltpu.roll(column, COLUMN_LANE, 1), packed[...])
    for n in range(3):
        at = plan.window_at + n * TILE
        edges[at : at + TILE, :] = pack(windows[16 * n : 16 * n + 16], WIN_K)
    for ref in (to_even, to_odd):
        at = sent.density
        ref[at : at + 3 * TILE, :] = column[: 3 * TILE]


def as_float(flag):
    return flag.astype(jnp.float32)


class Sides:
    def __init__(self, axis):
        index = lax.axis_index(axis)
        last = lax.axis_size(axis) - 1
        odd = lax.rem(index, 2)
        even = 1 - odd
        self.left = as_float(odd), as_float(even * (index > 0).astype(jnp.int32))
        self.right = as_float(even), as_float(odd * (index < last).astype(jnp.int32))

    @staticmethod
    def of(side, even, odd, at, count):
        return side[0] * even[at : at + count, :] + side[1] * odd[at : at + count, :]


class Rows:
    def __init__(self, depth, own, from_even, from_odd):
        self.sides = Sides("gx")
        self.sent = Sent(depth)
        self.depth = depth
        self.low, self.base = near_layers(depth)
        self.own = own
        self.even, self.odd = from_even, from_odd

    def of(self, row, at, count):
        side = self.sides.left if row < 0 else self.sides.right
        return self.sides.of(side, self.even, self.odd, at, count)

    def full(self, name, c, row):
        if 0 <= row < 4:
            return self.own[name][c, row]
        distance = -row if row < 0 else row - 3
        if (name, c, distance) not in self.sent.full:
            return jnp.zeros((self.depth, LANES), jnp.float32)
        return self.of(row, self.sent.full[name, c, distance], self.depth)

    def window(self, name, c, row):
        sent = self.sent
        if 0 <= row < 4:
            low = self.low - self.base if name in ("e", "h") else self.low
            return self.own[name][c, row, low : low + TILE, :]
        distance = -row if row < 0 else row - 3
        if (name, c, distance) in sent.full:
            return self.of(row, sent.full[name, c, distance] + self.low, TILE)
        if (name, c, distance) not in sent.pieces:
            return jnp.zeros((TILE, LANES), jnp.float32)
        at, count, from_left, from_right = sent.pieces[name, c, distance]
        at -= self.depth // 2 - self.low + (from_left if row < 0 else from_right)
        return self.of(row, at, TILE)


def combine_kernel(depth, odd, even, halo):
    plan = Edges(depth)
    sides = Sides("gy")
    for at, end, width in ((0, plan.window_at, FULL_K), (plan.window_at, plan.rows, WIN_K)):
        lane = lane_index(end - at)
        from_left = lax.rem(lane, 2 * width) >= width
        if at == 0:
            beside = (lane >= COLUMN_LANE - COLUMN_K) & (lane < COLUMN_LANE + COLUMN_K)
            from_left = jnp.where(beside, (lane < COLUMN_LANE).astype(jnp.int32), from_left.astype(jnp.int32)) == 1
        left = sides.of(sides.left, even, odd, at, end - at)
        right = sides.of(sides.right, even, odd, at, end - at)
        halo[at:end, :] = jnp.where(from_left, left, right)


def columns_kernel(depth, den, reg, from_odd, from_even, halo, halo_odd, halo_even, columns, far):
    sent = Sent(depth)
    sides = Sides("gx")
    odd = as_float(lax.rem(lax.axis_index("gx"), 2))
    count = 3 * TILE

    def beside(ref):
        return pltpu.roll(ref[0:count, :], LANES - COLUMN_LANE, 1)

    def within(ref):
        return ref[sent.density : sent.density + count, :]

    for lane, (own, even, away) in enumerate(
        ((None, within(from_even), within(from_odd)), (beside(halo), beside(halo_even), beside(halo_odd)))
    ):
        lanes = pl.ds(lane * LANES, LANES)
        below = sides.left[0] * even + sides.left[1] * away
        above = sides.right[0] * even + sides.right[1] * away
        zero_row = jnp.zeros((1, LANES), jnp.float32)
        mate = 2 * TILE
        for n in range(3):
            if own is None:
                here = den[n] if n < 2 else reg[...].astype(jnp.float32)
            else:
                here = own[4 * n : 4 * n + 4]
            to = 16 * n
            columns[to : to + 1, lanes] = zero_row
            columns[to + 15 : to + 16, lanes] = zero_row
            first = last = zero_row
            if n < 2:
                first = sides.left[1] * away[mate + 4 * n + 3 : mate + 4 * n + 4]
                last = sides.right[1] * away[mate + 4 * n : mate + 4 * n + 1]
                far[2 * n + lane : 2 * n + lane + 1, :] = (1.0 - odd) * below[4 * n + 3 : 4 * n + 4] + odd * above[4 * n : 4 * n + 1]
            columns[to + 1 : to + 2, lanes] = first
            columns[to + 2 : to + 6, lanes] = below[4 * n : 4 * n + 4]
            columns[to + 6 : to + 10, lanes] = here
            columns[to + 10 : to + 14, lanes] = above[4 * n : 4 * n + 4]
            columns[to + 14 : to + 15, lanes] = last
    far[4:8, :] = jnp.zeros((4, LANES), jnp.float32)


def up_z(block):
    depth = block.shape[0]
    moved = pltpu.roll(block, depth - 1, 0)
    if depth == TILE:
        return moved - block
    edge = lax.broadcasted_iota(jnp.int32, block.shape, 0) == depth - 1
    return jnp.where(edge, 0.0, moved) - block


def down_z(block):
    moved = pltpu.roll(block, 1, 0)
    if block.shape[0] == TILE:
        return block - moved
    edge = lax.broadcasted_iota(jnp.int32, block.shape, 0) == 0
    return block - jnp.where(edge, 0.0, moved)


def up_y(block):
    return pltpu.roll(block, block.shape[1] - 1, 1) - block


def down_y(block):
    return block - pltpu.roll(block, 1, 1)


def curl_up(here, after):
    x, y, z = here
    return (up_y(z) - up_z(y), up_z(x) - (after[2] - z), (after[1] - y) - up_y(x))


def curl_down(here, before):
    x, y, z = here
    return (down_y(z) - down_z(y), down_z(x) - (z - before[2]), (y - before[1]) - down_y(x))


def blur(block):
    table = kernel_table(RAD)
    lanes, count = block.shape[1], block.shape[0]
    sums = [block]
    for b in range(1, RAD + 1):
        sums.append(pltpu.roll(block, b, 1) + pltpu.roll(block, lanes - b, 1))
    total = None
    for a in range(RAD + 1):
        part = sum(float(table[RAD + a, RAD + b]) * sums[b] for b in range(RAD + 1))
        if a:
            part = pltpu.roll(part, a, 0) + pltpu.roll(part, count - a, 0)
        total = part if total is None else total + part
    return total


class Halos:
    def __init__(self, depth, x_sides, own, even, odd):
        self.depth = depth
        self.plan = Edges(depth)
        self.x_sides = x_sides
        self.own, self.even, self.odd = own, even, odd

    def of(self, row, at, count):
        if 0 <= row < 4:
            return self.own[at : at + count, :]
        side = self.x_sides.left if row < 0 else self.x_sides.right
        return self.x_sides.of(side, self.even, self.odd, at, count)

    def full(self, name, c, row):
        return unroll(self.of(row, 0, self.depth), self.plan.full_slot(name, c, row) * 2 * FULL_K)

    def window(self, name, c, row):
        at, slot = self.plan.window_slot(name, c, row)
        return unroll(self.of(row, self.plan.window_at + at, TILE), slot * 2 * WIN_K)


def unroll(block, shift):
    return pltpu.roll(block, LANES - shift, 1) if shift else block


class Coefficients:
    def __init__(self, region, densities):
        self.design = (region == 2.0).astype(jnp.float32)
        self.absorbing = (region == 1.0).astype(jnp.float32)
        self.source = (region == 3.0).astype(jnp.float32)
        self.inverse, self.slope = [], []
        for density in densities:
            inner = jnp.tanh(SHARP * (blur(density) - LEVEL))
            projected = (CREST + inner) / SCALE
            self.slope.append(SHARP * (1.0 - inner * inner) / SCALE)
            self.inverse.append(1.0 / (1.0 + CONTRAST * self.design * projected))
        damp = ABSORB * self.absorbing
        self.keep = (1.0 - damp) / (1.0 + damp)
        self.gain = COURANT / (1.0 + damp)


def inside_masks(x_sides, y_sides):
    lane = lane_index(TILE, 2 * LANES)
    inside = jnp.where(lane < LANES, 1.0, jnp.where(lane < LANES + LANES // 2, sum(y_sides.right), sum(y_sides.left)))
    return {"own": inside, "below": inside * sum(x_sides.left), "above": inside * sum(x_sides.right)}


def where_row(row):
    return "own" if 0 <= row < 4 else ("below" if row < 0 else "above")


def spread(block, row, count=TILE):
    at = row + DEN_BASE
    return jnp.broadcast_to(block[at : at + 1, :], (count, block.shape[1]))


def near_kernel(
    depth, columns, far, done_e, done_h, near,
    out_grad, out_e, out_h,
    grad, ratio_rows, sems,
):
    copies = [
        pltpu.make_async_copy(done_e, out_e, sems.at[0]),
        pltpu.make_async_copy(done_h, out_h, sems.at[1]),
        pltpu.make_async_copy(grad, out_grad, sems.at[2]),
    ]
    copies[0].start()
    copies[1].start()
    wide = 2 * LANES
    centre = depth // 2
    low = near_layers(depth)[0]

    def given(n, row):
        return [near[n, c, row + 3] for c in range(3)]

    odd = lax.rem(lax.axis_index("gx"), 2)
    far_at = jnp.where(odd == 1, DEN_BASE - 5, DEN_BASE + 8)
    at_far = lax.broadcasted_iota(jnp.int32, (16, wide), 0) == far_at
    densities = []
    for layer in range(2):
        row = jnp.concatenate([far[2 * layer : 2 * layer + 1, :], far[2 * layer + 1 : 2 * layer + 2, :]], 1)
        densities.append(jnp.where(at_far, jnp.broadcast_to(row, (16, wide)), columns[16 * layer : 16 * layer + 16, :]))
    known = Coefficients(columns[32:48, :], densities)
    inverse, slope, design, source = known.inverse, known.slope, known.design, known.source
    keep_col, gain_col = known.keep, known.gain
    masks = inside_masks(Sides("gx"), Sides("gy"))
    steps = {key: COURANT * value for key, value in masks.items()}

    sub = lax.broadcasted_iota(jnp.int32, (TILE, wide), 0) + low

    def layered(row):
        first, second = spread(inverse[0], row), spread(inverse[1], row)
        return jnp.where(sub == centre, first, jnp.where(sub == centre + 1, second, 1.0))

    keep_win = {row: spread(keep_col, row) for row in range(-3, 7)}
    layer_win = {row: layered(row) for row in range(-3, 7)}
    gain_win = {row: spread(gain_col, row) * layer_win[row] * masks[where_row(row)] for row in range(-3, 7)}
    source_plane = (sub == centre - 1).astype(jnp.float32)
    h1, e1, h2, drive1, drive2 = {}, {}, {}, {}, {}

    def minus_step(base, curl, row):
        step = steps[where_row(row)]
        return [b - step * c for b, c in zip(base, curl)]

    for row in range(-3, 7):
        h1[row], drive1[row] = given(0, row), given(1, row)
        e1[row] = [kept + gain_win[row] * d for kept, d in zip(given(2, row), drive1[row])]
    for row in range(-3, 6):
        h2[row] = minus_step(h1[row], curl_up(e1[row], e1[row + 1]), row)
    for row in range(-2, 6):
        drive2[row] = list(curl_down(h2[row], h2[row - 1]))
        drive2[row][2] = drive2[row][2] - math.sin(OMEGA * 2.0) * source_plane * spread(source, row)
    a2 = {row: given(3, row) for row in range(-3, 7)}
    ga_win = {row: [gain_win[row] * v for v in a2[row]] for row in range(-3, 7)}
    bh_win = {}
    for row in range(-3, 6):
        mask = masks[where_row(row)]
        curl = curl_up(ga_win[row], ga_win[row + 1])
        bh_win[row] = [v + mask * d for v, d in zip(given(4, row), curl)]
    ratio_rows[...] = jnp.zeros(ratio_rows.shape, jnp.float32)
    for row in range(-2, 6):
        a1 = minus_step(
            [keep_win[row] * v for v in a2[row]], curl_down(bh_win[row], bh_win[row - 1]), row
        )
        total = sum(a2[row][c] * drive2[row][c] + a1[c] * drive1[row][c] for c in range(3))
        for layer in range(2):
            at = centre + layer - low
            ratio_rows[layer, row + DEN_BASE : row + DEN_BASE + 1, :] = total[at : at + 1, :]
    for layer in range(2):
        sensitivity = -ratio_rows[layer] * gain_col * inverse[layer] * inverse[layer]
        smoothed = blur(CONTRAST * design * sensitivity * slope[layer])
        grad[layer] = smoothed[DEN_BASE : DEN_BASE + 4, :LANES]
    copies[2].start()
    for copy in copies:
        copy.wait()


def full_kernel(
    depth, e, h, ae, ah, from_even, from_odd, halo, halo_even, halo_odd, columns,
    out_e, out_h, near,
    ga, bh, be, gb,
):
    rows = Rows(depth, {"e": e, "h": h, "ae": ae, "ah": ah}, from_even, from_odd)
    halos = Halos(depth, rows.sides, halo, halo_even, halo_odd)
    wide = 2 * LANES
    centre = depth // 2

    def full(name, c, row):
        return jnp.concatenate([rows.full(name, c, row), halos.full(name, c, row)], 1)

    known = Coefficients(columns[32:48, :], [columns[16 * layer : 16 * layer + 16, :] for layer in range(2)])
    inverse, absorbing = known.inverse, known.absorbing
    masks = inside_masks(rows.sides, Sides("gy"))
    steps = {key: COURANT * value for key, value in masks.items()}

    def window(name, c, row):
        return jnp.concatenate([rows.window(name, c, row), halos.window(name, c, row)], 1)

    sub = lax.broadcasted_iota(jnp.int32, (TILE, wide), 0) + rows.low
    at_source = (sub == centre - 1).astype(jnp.float32) * math.sin(OMEGA)
    fields, magnetic = {}, {}
    for row in range(-4, 8):
        fields[row] = [window("e", c, row) for c in range(3)]
    for row in range(-4, 7):
        curl = curl_up(fields[row], fields[row + 1])
        magnetic[row] = [window("h", c, row) - steps[where_row(row)] * curl[c] for c in range(3)]
    for row in range(-3, 7):
        drive = list(curl_down(magnetic[row], magnetic[row - 1]))
        drive[2] = drive[2] - at_source * spread(known.source, row)
        keep = spread(known.keep, row)
        for c in range(3):
            near[0, c, row + 3] = magnetic[row][c]
            near[1, c, row + 3] = drive[c]
            near[2, c, row + 3] = keep * fields[row][c]
            near[3, c, row + 3] = window("ae", c, row)
            if row < 6:
                near[4, c, row + 3] = window("ah", c, row)

    z = lax.broadcasted_iota(jnp.int32, (depth, wide), 0)
    zf = z.astype(jnp.float32)
    margin = float(depth // 8)
    ramp = jnp.maximum(jnp.maximum((margin - zf) / margin, (zf - (depth - 1 - margin)) / margin), 0.0)
    open_damp = ABSORB * ramp * ramp
    full_damp = open_damp + ABSORB
    gain_open, gain_abs = COURANT / (1.0 + open_damp), COURANT / (1.0 + full_damp)
    keep_open, keep_abs = (1.0 - open_damp) / (1.0 + open_damp), (1.0 - full_damp) / (1.0 + full_damp)

    def coefficient(row):
        flag = spread(absorbing, row, depth) > 0.5
        layers = jnp.where(
            z == centre,
            spread(inverse[0], row, depth),
            jnp.where(z == centre + 1, spread(inverse[1], row, depth), 1.0),
        )
        return jnp.where(flag, keep_abs, keep_open), jnp.where(flag, gain_abs, gain_open) * layers

    def stretch(block):
        return jnp.broadcast_to(block[:1, :], (depth, wide))

    masks = {key: stretch(value) for key, value in masks.items()}
    steps = {key: stretch(value) for key, value in steps.items()}

    for row in range(-2, 6):
        keep, gain = coefficient(row)
        for c in range(3):
            value = full("ae", c, row)
            ga[c, row + 2] = gain * value
            if -1 <= row <= 4:
                be[c, row + 1] = keep * value
    for row in range(-2, 5):
        curl = curl_up([ga[c, row + 2] for c in range(3)], [ga[c, row + 3] for c in range(3)])
        for c in range(3):
            bh[c, row + 2] = full("ah", c, row) + masks[where_row(row)] * curl[c]
    for row in range(-1, 5):
        keep, gain = coefficient(row)
        curl = curl_down([bh[c, row + 2] for c in range(3)], [bh[c, row + 1] for c in range(3)])
        for c in range(3):
            value = be[c, row + 1] - steps[where_row(row)] * curl[c]
            be[c, row + 1] = keep * value
            gb[c, row + 1] = gain * value
    for row in range(-1, 4):
        curl = curl_up([gb[c, row + 1] for c in range(3)], [gb[c, row + 2] for c in range(3)])
        for c in range(3):
            value = bh[c, row + 2] + masks[where_row(row)] * curl[c]
            bh[c, row + 2] = value
            if row >= 0:
                out_h[c, row] = value[:, :LANES]
    for row in range(4):
        curl = curl_down([bh[c, row + 2] for c in range(3)], [bh[c, row + 1] for c in range(3)])
        for c in range(3):
            out_e[c, row] = be[c, row + 1][:, :LANES] - COURANT * curl[c][:, :LANES]


def per_device(density, e_field, h_field, adj_e, adj_h, region):
    depth = e_field.shape[2]
    sent, plan = Sent(depth), Edges(depth)
    f32 = jnp.float32
    params = pltpu.CompilerParams(vmem_limit_bytes=32 * 1024 * 1024)
    shape = jax.ShapeDtypeStruct
    near = e_field.shape[:2] + (2 * TILE, LANES)
    mate_den = pair_permute(density, x_even)
    own = pl.pallas_call(
        functools.partial(load_kernel, depth),
        out_shape=(
            pltpu.VMEM(density.shape, f32),
            pltpu.VMEM(near, f32),
            pltpu.VMEM(near, f32),
            pltpu.VMEM(adj_e.shape, f32),
            pltpu.VMEM(adj_h.shape, f32),
            pltpu.VMEM(region.shape, region.dtype),
            pltpu.VMEM((depth, LANES), f32),
        ),
        in_specs=[pl.BlockSpec(memory_space=pltpu.HBM)] * 6,
        scratch_shapes=[pltpu.SemaphoreType.DMA((6,))],
        compiler_params=pltpu.CompilerParams(vmem_limit_bytes=LOAD_VMEM),
        name="load",
    )(density, e_field, h_field, adj_e, adj_h, region)
    fields = own[1:5]
    edges, to_even, to_odd = pl.pallas_call(
        functools.partial(first_kernel, depth),
        out_shape=(
            shape((plan.rows, LANES), f32),
            shape((sent.rows, LANES), f32),
            shape((sent.rows, LANES), f32),
        ),
        compiler_params=params,
        name="first",
    )(*own, mate_den)
    edges_even = pair_permute(edges, y_even)
    edges_odd = pair_permute(edges, y_odd)
    from_odd = pair_permute(to_odd, x_ring)
    from_even = pair_permute(to_even, x_even)
    halo = pl.pallas_call(
        functools.partial(combine_kernel, depth),
        out_shape=shape((plan.rows, LANES), f32),
        compiler_params=params,
        name="combine",
    )(edges_odd, edges_even)
    halo_odd = pair_permute(halo, x_ring)
    halo_even = pair_permute(halo, x_even)
    wide = 2 * LANES
    columns, far = pl.pallas_call(
        functools.partial(columns_kernel, depth),
        out_shape=(shape((48, wide), f32), shape((TILE, LANES), f32)),
        compiler_params=params,
        name="columns",
    )(own[0], own[5], from_odd, from_even, halo, halo_odd, halo_even)
    far = pair_permute(far, x_even)
    done = pl.pallas_call(
        functools.partial(full_kernel, depth),
        out_shape=(
            pltpu.VMEM(e_field.shape, f32),
            pltpu.VMEM(e_field.shape, f32),
            pltpu.VMEM((5, 3, 10, TILE, wide), f32),
        ),
        scratch_shapes=[
            pltpu.VMEM((3, 8, depth, wide), f32),
            pltpu.VMEM((3, 7, depth, wide), f32),
            pltpu.VMEM((3, 6, depth, wide), f32),
            pltpu.VMEM((3, 6, depth, wide), f32),
        ],
        compiler_params=params,
        name="full",
    )(*fields, from_even, from_odd, halo, halo_even, halo_odd, columns)
    return pl.pallas_call(
        functools.partial(near_kernel, depth),
        out_shape=(shape(density.shape, f32), shape(e_field.shape, f32), shape(e_field.shape, f32)),
        out_specs=[pl.BlockSpec(memory_space=pltpu.HBM)] * 3,
        scratch_shapes=[
            pltpu.VMEM(density.shape, f32),
            pltpu.VMEM((2, 16, wide), f32),
            pltpu.SemaphoreType.DMA((3,)),
        ],
        compiler_params=params,
        name="near",
    )(columns, far, *done)


def solution(mesh):
    field = P(None, "gx", None, "gy")
    design = P(None, "gx", "gy")
    return jax.shard_map(
        per_device,
        mesh=mesh,
        in_specs=(design, field, field, field, field, P("gx", "gy")),
        out_specs=(design, field, field),
        check_vma=False,
    )
```
